256 devices in a mesh: horiz: 32 (over x, z), lev: 8 (over y, core).
Axes of the slice: x: 4, y: 4, z: 8, core: 2. Of those that a mesh axis runs over, the one named last changes fastest.
Arguments:
- perturb: bfloat16 [16, 256, 16384], P('lev', None, 'horiz'), may hold values from -6 to 6
- mean_state: float32 [16, 16384], P('lev', 'horiz'), may hold values from -6 to 6
- obs_value: float32 [2, 1024], replicated, may hold values from -8 to 8
- obs_var: float32 [2, 1024], replicated, may hold values from 0.3 to 3
- obs_weight: float32 [2, 1024], replicated, may hold values from 0 to 1
- obs_tile: int32 [2, 1024], replicated, may hold values from 0 to 31, as said below
- obs_col: int32 [2, 1024], replicated, may hold values from 0 to 511
- obs_level: int32 [2, 1024], replicated, may hold values from 0 to 15
- loc_horiz: float32 [2, 32, 1024], replicated, may hold values from 0.2 to 1
- loc_vert: float32 [2, 16, 1024], replicated, may hold values from 0.2 to 1
Outputs:
- perturb_out: bfloat16 [16, 256, 16384], P('lev', None, 'horiz')
- mean_out: float32 [16, 16384], P('lev', 'horiz')
The draws below stay inside these ranges and needn't reach their ends.
Inputs may be any that keep to these rules, and one draw needn't show every extreme that they name: `obs_tile`: in each batch every tile holds the site of at least one observation at its last column.
All inputs are finite; a program needn't handle non-finite values.
Results may differ from the reference program's by a relative error of at most 0.0051.
Values sent between devices are 32-bit elements; how exact they have to be, the bound alone decides.
A program may use at most 128 MiB of HBM per device.

```python
import math
import jax
import jax.numpy as jnp
from jax import lax

MEMBERS = 256
OBS = 1024
BATCHES = 2
COL_DEV = 512
NTILES = 32
COLUMNS = 16384
LEVELS = 16


def site_draw(key, batch_no):
    base = jax.random.fold_in(key, 100 + batch_no)
    keys = jax.random.split(base, 6)
    every_tile = jax.random.permutation(keys[0], NTILES).astype(jnp.int32)
    lower = jnp.minimum(jax.random.randint(keys[1], (OBS,), 0, NTILES), jax.random.randint(keys[2], (OBS,), 0, NTILES))
    relabel = jax.random.permutation(keys[3], NTILES).astype(jnp.int32)
    skewed = relabel[lower]
    tiles = jnp.concatenate([every_tile, skewed[NTILES:]]).astype(jnp.int32)
    random_cols = jax.random.randint(keys[4], (OBS,), 0, COL_DEV)
    cols = jnp.concatenate([jnp.full((NTILES,), COL_DEV - 1, jnp.int32), random_cols[NTILES:].astype(jnp.int32)])
    order = jax.random.permutation(keys[5], OBS)
    return (tiles[order], cols[order])


def draw_obs_tile(key, part):
    return jnp.stack([site_draw(key, batch_no)[0] for batch_no in range(BATCHES)])


def draw_obs_col(key, part):
    return jnp.stack([site_draw(key, batch_no)[1] for batch_no in range(BATCHES)])


def touch_ends(drawn, key, smallest, largest):
    extent = drawn.shape
    spot = [jax.random.randint(jax.random.fold_in(key, axis), (), 0, extent[axis]) for axis in range(len(extent))]
    drawn = drawn.at[tuple(spot)].set(smallest)
    longest = extent.index(max(extent))
    spot[longest] = (spot[longest] + 1) % extent[longest]
    return drawn.at[tuple(spot)].set(largest)


def shard_levels(stream_key, shape, cuts, smallest, high):
    def one(axis_at, shards_of):
        heights = jax.random.uniform(jax.random.fold_in(jax.random.fold_in(stream_key, 6), axis_at), (shards_of,), jnp.float32, smallest / len(cuts), high / len(cuts))
        return jnp.repeat(jnp.exp(heights), shape[axis_at] // shards_of).reshape((-1,) + (1,) * (len(shape) - axis_at - 1))

    gain = one(*cuts[0])
    for cut in cuts[1:]:
        gain = gain * one(*cut)
    return gain


def bell_draw(key, shape, scale, reach, pieces=(), held_as=jnp.bfloat16):
    entries = jax.random.normal(key, shape, jnp.float32) * scale
    if len(pieces) > 0:
        entries = shard_levels(key, shape, pieces, -0.22, 0.18) * entries
    return jnp.clip(entries, min=-reach, max=reach).astype(held_as)


def setup_inputs(seed: int = 0) -> dict:
    key_of = jax.random.split(jax.random.key(seed), 11)
    perturb = bell_draw(key_of[0], (LEVELS, MEMBERS, COLUMNS), 1.0, 6.0, ((0, 8), (2, 32)))
    mean_state = bell_draw(key_of[1], (LEVELS, COLUMNS), 1.0, 6.0, ((0, 8), (1, 32)), jnp.float32)
    obs_value = bell_draw(key_of[2], (BATCHES, OBS), 1.5, 8.0, (), jnp.float32)
    obs_var = jnp.clip(jnp.exp(jax.random.uniform(key_of[3], (BATCHES, OBS), jnp.float32, math.log(0.3), math.log(3.0))), 0.3, 3.0)
    obs_weight = jnp.clip(jax.random.uniform(key_of[4], (BATCHES, OBS), jnp.float32, 0.0, 1.0), 0.0, 1.0)
    obs_tile = draw_obs_tile(jax.random.fold_in(key_of[10], 71), 0)
    obs_col = draw_obs_col(jax.random.fold_in(key_of[10], 71), 0)
    obs_level = touch_ends(jax.random.randint(key_of[7], (BATCHES, OBS), 0, LEVELS), jax.random.fold_in(key_of[7], 1), 0, LEVELS - 1).astype(jnp.int32)
    loc_horiz = jnp.clip(jax.random.uniform(key_of[8], (BATCHES, NTILES, OBS), jnp.float32, 0.2, 1.0), 0.2, 1.0)
    loc_vert = jnp.clip(jax.random.uniform(key_of[9], (BATCHES, LEVELS, OBS), jnp.float32, 0.2, 1.0), 0.2, 1.0)
    return {"perturb": perturb, "mean_state": mean_state, "obs_value": obs_value, "obs_var": obs_var, "obs_weight": obs_weight, "obs_tile": obs_tile, "obs_col": obs_col, "obs_level": obs_level, "loc_horiz": loc_horiz, "loc_vert": loc_vert}


def solve_batch(panel_rows, site_means, value_row, var_row, members):
    innovation = value_row - site_means
    innov_cov = jnp.dot(panel_rows, panel_rows.T, precision=lax.Precision.HIGHEST) / (members - 1) + jnp.diag(var_row)
    factor = jnp.linalg.cholesky(innov_cov)
    half_solve = lax.linalg.triangular_solve(factor, innovation[:, None], left_side=True, lower=True)
    weights = lax.linalg.triangular_solve(factor, half_solve, left_side=True, lower=True, transpose_a=True)[:, 0]
    shifted = factor + jnp.diag(jnp.sqrt(var_row))
    left_solve = lax.linalg.triangular_solve(shifted, panel_rows, left_side=True, lower=True)
    gain_rows = lax.linalg.triangular_solve(factor, left_solve, left_side=True, lower=True, transpose_a=True)
    return (weights, gain_rows)

def reference(perturb, mean_state, obs_value, obs_var, obs_weight, obs_tile, obs_col, obs_level, loc_horiz, loc_vert):
    for batch_no in range(BATCHES):
        site_cell = obs_tile[batch_no] * COL_DEV + obs_col[batch_no]
        next_cell = (site_cell + 1) % COLUMNS
        fraction = obs_weight[batch_no]
        site_lev = obs_level[batch_no]
        left_vals = perturb[site_lev, :, site_cell].astype(jnp.float32)
        right_vals = perturb[site_lev, :, next_cell].astype(jnp.float32)
        panel_rows = (1.0 - fraction)[:, None] * left_vals + fraction[:, None] * right_vals
        site_means = (1.0 - fraction) * mean_state[site_lev, site_cell] + fraction * mean_state[site_lev, next_cell]
        weights, gain_rows = solve_batch(panel_rows, site_means, obs_value[batch_no], obs_var[batch_no], MEMBERS)
        rows_half = panel_rows.astype(jnp.bfloat16)
        gain_half = gain_rows.astype(jnp.bfloat16)
        slabs = perturb.reshape(LEVELS, MEMBERS, NTILES, COL_DEV).transpose(0, 2, 1, 3).reshape(LEVELS * NTILES, MEMBERS, COL_DEV)
        mean_rows = mean_state.reshape(LEVELS * NTILES, COL_DEV)

        def one_block(item):
            slab_rows, mean_row, index = item
            level_no = index // NTILES
            tile_no = index % NTILES
            spread = jnp.dot(slab_rows.T.astype(jnp.float32), rows_half.T.astype(jnp.float32), preferred_element_type=jnp.float32) / (MEMBERS - 1)
            damping = loc_horiz[batch_no, tile_no] * loc_vert[batch_no, level_no]
            damped = spread * damping[None, :]
            tile_gain = damped.astype(jnp.bfloat16)
            mean_new = mean_row + jnp.dot(damped, weights, precision=lax.Precision.HIGHEST)
            increment = jnp.dot(gain_half.T.astype(jnp.float32), tile_gain.T.astype(jnp.float32), preferred_element_type=jnp.float32)
            updated = (slab_rows.astype(jnp.float32) - increment).astype(jnp.bfloat16)
            return (updated, mean_new)
        new_slabs, new_means = lax.map(one_block, (slabs, mean_rows, jnp.arange(LEVELS * NTILES, dtype=jnp.int32)))
        perturb = new_slabs.reshape(LEVELS, NTILES, MEMBERS, COL_DEV).transpose(0, 2, 1, 3).reshape(LEVELS, MEMBERS, COLUMNS)
        mean_state = new_means.reshape(LEVELS, COLUMNS)
    return (perturb, mean_state)
```

```python
import functools
import jax
import jax.numpy as jnp
from jax import lax
from jax.experimental import pallas as pl
from jax.experimental.pallas import tpu as pltpu
from jax.sharding import PartitionSpec as P

F32 = jnp.float32
BF16 = jnp.bfloat16
HIGHEST = lax.Precision.HIGHEST
MESH = pl.DeviceIdType.MESH
B = 128
Q = 32
NT = ((1,), (1,))
TN = ((0,), (0,))
NN = ((1,), (0,))


def mm(a, b, dims=NN):
    return lax.dot_general(a, b, (dims, ((), ())), precision=HIGHEST, preferred_element_type=F32)


def mm16(a, b):
    return jnp.dot(a, b, preferred_element_type=F32)


def columns_of(rows):
    return jnp.concatenate([rows] * 16, axis=0).T


def rows_at(i):
    return pl.ds(pl.multiple_of(i * B, B), B)


def gather_sites(batch, x_ref, xm_ref, tile_ref, col_ref, level_ref, frac_ref, out_ref):
    levels, members, cols = x_ref.shape
    tiles = 32
    my_tile = lax.axis_index("horiz")
    first = lax.axis_index("lev") * levels
    row = lax.broadcasted_iota(jnp.int32, (8, B), 0)
    width = 2 * B
    cells = lax.broadcasted_iota(jnp.int32, (cols, width), 0)
    parts = []
    for lev in range(levels):
        xm = xm_ref[lev : lev + 1, :]
        hi = xm.astype(BF16).astype(F32)
        mid = (xm - hi).astype(BF16).astype(F32)
        low = xm - hi - mid
        r16 = lax.broadcasted_iota(jnp.int32, (16, cols), 0)
        stack = jnp.where(r16 == 0, hi, jnp.where(r16 == 1, mid, jnp.where(r16 == 2, low, 0.0)))
        parts.append(stack.astype(BF16))
    for jb in range(4):
        lanes = slice(jb * width, (jb + 1) * width)
        tile = tile_ref[batch : batch + 1, lanes]
        col = col_ref[batch : batch + 1, lanes]
        level = level_ref[batch : batch + 1, lanes]
        frac = frac_ref[batch : batch + 1, lanes]
        wraps = col == cols - 1
        next_tile = jnp.where(wraps, jnp.where(tile == tiles - 1, 0, tile + 1), tile)
        next_col = jnp.where(wraps, 0, col + 1)
        vals = []
        for t, c in ((tile, col), (next_tile, next_col)):
            v = jnp.zeros((members, width), F32)
            m = jnp.zeros((16, width), F32)
            for lev in range(levels):
                pos = jnp.where((t == my_tile) & (level == first + lev), c, -1)
                hot = jnp.where(cells == pos, 1.0, 0.0).astype(BF16)
                v = v + mm16(x_ref[lev], hot)
                m = m + mm16(parts[lev], hot)
            vals.append((v, jnp.sum(m[0:8], axis=0, keepdims=True)))
        site = (1.0 - frac) * vals[0][0] + frac * vals[1][0]
        mean = (1.0 - frac) * vals[0][1] + frac * vals[1][1]
        for core in range(2):
            half = slice(core * B, (core + 1) * B)
            out_ref[core, jb, 0:32] = site[:, half].reshape(32, 8, B)
            out_ref[core, jb, 32] = jnp.where(row == 0, mean[:, half], 0.0)


def gather_kernel(x_ref, xm_ref, tile_ref, col_ref, level_ref, frac_ref, out_ref):
    gather_sites(0, x_ref, xm_ref, tile_ref, col_ref, level_ref, frac_ref, out_ref)


def sum_kernel(c_ref, o_ref, r0, a0, r1, a1, r2, a2, r3, a3, send, recv):
    horiz = lax.axis_index("horiz")
    lev = lax.axis_index("lev")
    x, z = horiz // 8, horiz % 8
    y, core = lev // 2, lev % 2

    def at(dx=0, dz=0, dy=0, dc=0):
        return (((x + dx) % 4) * 8 + (z + dz) % 8, ((y + dy) % 4) * 2 + (core + dc) % 2)

    peers = (
        [at(dc=1)]
        + [at(dy=k) for k in range(1, 4)]
        + [at(dx=k) for k in range(1, 4)]
        + [at(dz=k) for k in range(1, 8)]
    )
    barrier = pltpu.get_barrier_semaphore()
    for peer in peers:
        pl.semaphore_signal(barrier, inc=1, device_id=peer, device_id_type=MESH)
    pl.semaphore_wait(barrier, len(peers))

    count = [0]

    def start(src, dst, peer):
        k = count[0]
        count[0] += 1
        copy = pltpu.make_async_remote_copy(
            src_ref=src, dst_ref=dst, send_sem=send.at[k], recv_sem=recv.at[k],
            device_id=peer, device_id_type=MESH,
        )
        copy.start()
        return copy

    sent = []
    other = 1 - core
    first = []
    for k in (1, 2, 3, 0):
        yk = (y + k) % 4
        first.append((yk, start(c_ref.at[other, yk], r0.at[yk], at(dc=1))))
    ys = []
    for k, (yk, copy) in zip((1, 2, 3, 0), first):
        copy.wait_recv()
        a0[yk] = c_ref[core, yk] + r0[yk]
        if k:
            ys.append(start(a0.at[yk], r1.at[k - 1], at(dy=k)))
    sent += [copy for _, copy in first]
    for copy in ys:
        copy.wait_recv()
    a1[...] = (a0[y] + r1[0]) + (r1[1] + r1[2])
    sent += ys
    xs = []
    for k in range(1, 4):
        xk = (x + k) % 4
        xs.append(start(a1.at[pl.ds(8 * xk, 8)], r2.at[k - 1, pl.ds(0, 8)], at(dx=k)))
        xs.append(start(a1.at[pl.ds(32, 1)], r2.at[k - 1, pl.ds(8, 1)], at(dx=k)))
    for copy in xs:
        copy.wait_recv()
    a2[0:8] = (a1[pl.ds(8 * x, 8)] + r2[0, 0:8]) + (r2[1, 0:8] + r2[2, 0:8])
    a2[8:9] = (a1[32:33] + r2[0, 8:9]) + (r2[1, 8:9] + r2[2, 8:9])
    sent += xs
    zs = []
    for k in range(1, 8):
        zk = (z + k) % 8
        zs.append(start(a2.at[pl.ds(zk, 1)], r3.at[k - 1, pl.ds(0, 1)], at(dz=k)))
        zs.append(start(a2.at[pl.ds(8, 1)], r3.at[k - 1, pl.ds(1, 1)], at(dz=k)))
    for copy in zs:
        copy.wait_recv()
    mine = a2[z]
    mean = a2[8]
    for k in range(7):
        mine = mine + r3[k, 0]
        mean = mean + r3[k, 1]
    o_ref[core, y, 8 * x + z] = mine
    o_ref[core, y, 32] = mean
    sent += zs
    zs = []
    for k in range(1, 8):
        spot = o_ref.at[core, y, pl.ds(8 * x + z, 1)]
        zs.append(start(spot, spot, at(dz=k)))
    for copy in zs:
        copy.wait_recv()
    xs = []
    for k in range(1, 4):
        spot = o_ref.at[core, y, pl.ds(8 * x, 8)]
        xs.append(start(spot, spot, at(dx=k)))
    for copy in xs:
        copy.wait_recv()
    spot = o_ref.at[core, y]
    ys = [start(spot, spot, at(dy=k)) for k in range(1, 4)]
    cs = [start(spot, spot, at(dc=1))]
    for k, copy in zip(range(1, 4), ys):
        copy.wait_recv()
        spot = o_ref.at[core, (y - k + 4) % 4]
        cs.append(start(spot, spot, at(dc=1)))
    for copy in cs:
        copy.wait_recv()
    for copy in sent + zs + xs + ys + cs:
        copy.wait_send()


COPIES = 4 + 3 + 6 + 14 + 7 + 3 + 3 + 4


def sum_over_devices(share):
    vm = pl.BlockSpec(memory_space=pltpu.VMEM)

    def buf(*shape):
        return pltpu.VMEM(shape + (8, B), F32)

    return pl.pallas_call(
        sum_kernel,
        out_shape=jax.ShapeDtypeStruct(share.shape, F32),
        in_specs=[vm],
        out_specs=vm,
        scratch_shapes=[
            buf(4, 33), buf(4, 33), buf(3, 33), buf(33), buf(3, 9), buf(9), buf(7, 2), buf(2),
            pltpu.SemaphoreType.DMA((COPIES,)),
            pltpu.SemaphoreType.DMA((COPIES,)),
        ],
        compiler_params=pltpu.CompilerParams(
            collective_id=0, has_side_effects=True, vmem_limit_bytes=24 * 2**20
        ),
    )(share)


def factor_block(s, dcol):
    nt = Q // 8
    row = lax.broadcasted_iota(jnp.int32, (8, B), 0)
    eye = jnp.where(
        lax.broadcasted_iota(jnp.int32, (B, B), 0) == lax.broadcasted_iota(jnp.int32, (B, B), 1),
        1.0,
        0.0,
    )
    m, a, z = s, eye, eye
    out_a, out_z = [], []
    for o in range(0, B, Q):
        w_t = [m[8 * t : 8 * t + 8] for t in range(nt)]
        a_t = [a[8 * t : 8 * t + 8] for t in range(nt)]
        z_t = [z[8 * t : 8 * t + 8] for t in range(nt)]
        cols = [
            [
                None if t < c // 8 else jnp.broadcast_to(w_t[t][:, o + c : o + c + 1], (8, B))
                for t in range(nt)
            ]
            for c in range(Q)
        ]
        for r in range(Q):
            tr, rr = r // 8, r % 8
            p = cols[r][tr][rr : rr + 1]
            rs = lax.rsqrt(p)
            l = [None if t < tr else cols[r][t] * rs for t in range(nt)]
            u = w_t[tr][rr : rr + 1] * rs
            av = a_t[tr][rr : rr + 1] * rs
            zv = z_t[tr][rr : rr + 1] / (p * rs + dcol[o + r : o + r + 1])
            for c in range(r + 1, Q):
                f = l[c // 8][c % 8 : c % 8 + 1]
                for t in range(c // 8, nt):
                    cols[c][t] = cols[c][t] - l[t] * f
            for t in range(tr, nt):
                lt = l[t] if t > tr else jnp.where(row > rr, l[t], 0.0)
                for rows, v in ((w_t, u), (a_t, av), (z_t, zv)):
                    new = rows[t] - lt * v
                    if t == tr:
                        new = jnp.where(row == rr, jnp.broadcast_to(v, (8, B)), new)
                    rows[t] = new
        u_b, a_b, z_b = (jnp.concatenate(rows, 0) for rows in (w_t, a_t, z_t))
        out_a.append(a_b)
        out_z.append(z_b)
        if o + Q < B:
            step = mm(u_b, jnp.concatenate([u_b, a_b, z_b], 1), TN)[o + Q :]
            m = m[Q:] - step[:, :B]
            a = a[Q:] - step[:, B : 2 * B]
            z = z[Q:] - step[:, 2 * B :]
    return jnp.concatenate(out_a, 0), jnp.concatenate(out_z, 0)


def analyse(
    panel_ref, x_ref, xm_ref, val_ref, var_ref, damp_ref, xo_ref, xmo_ref,
    a_ref, yb_ref, p_ref, qs_ref, s_ref, linv_ref, minv_ref, t1_ref, aq_ref, qv_ref, lz_ref,
    wl_ref, d_ref, vcol_ref, w_ref, gt_ref, k_ref,
):
    levels, members, cols = x_ref.shape
    n = a_ref.shape[0]
    nb = n // B
    c = 1.0 / (members - 1.0) ** 0.5

    def square(k):
        return lax.broadcasted_iota(jnp.int32, (k, k), 0) == lax.broadcasted_iota(
            jnp.int32, (k, k), 1
        )

    eye_m = jnp.where(square(members), 1.0, 0.0)
    diag = square(B)
    for i in range(nb):
        y_i = panel_ref[i % 2, i // 2, 0:32].reshape(members, B).T
        a_ref[i * B : (i + 1) * B] = y_i * c
        yb_ref[i * B : (i + 1) * B] = y_i.astype(BF16)
        d_ref[i : i + 1] = val_ref[i : i + 1] - panel_ref[i % 2, i // 2, 32][0:1]
    var_cols = columns_of(var_ref[...])
    for i in range(nb):
        vcol_ref[i] = jnp.broadcast_to(var_cols[:, i : i + 1], (B, B))
    p_ref[...] = eye_m
    qs_ref[0] = eye_m * (1.0 / c)
    a_0 = a_ref[0:B]
    s_ref[...] = mm(a_0, a_0, NT) + jnp.where(diag, var_ref[0:1], 0.0)
    for ref in (linv_ref, minv_ref, t1_ref, aq_ref, qv_ref):
        ref[...] = jnp.zeros_like(ref)

    def finish_previous(i):
        linv, minv, t1 = linv_ref[...], minv_ref[...], t1_ref[...]
        ip = jnp.maximum(i - 1, 0)
        v = mm(linv, t1)
        z = mm(minv, aq_ref[...])
        lz_ref[rows_at(i)] = mm(linv, z, TN)
        p = p_ref[...] - mm(v, v, TN)
        q = qs_ref[ip] - mm(v, z, TN)
        qv = qv_ref[...]
        rhs = d_ref[pl.ds(ip, 1)] - mm(qv, a_ref[rows_at(ip)], NT)
        qv = qv + mm(mm(rhs, linv, NT), v)
        return p, q, qv

    def step(i, carry):
        p, q, qv = finish_previous(i)
        i_next = jnp.minimum(i + 1, nb - 1)
        a_i = a_ref[rows_at(i)]
        a_n = a_ref[rows_at(i_next)]
        t1 = mm(a_i, p)
        t1_n = mm(a_n, p)
        s_nn = mm(t1_n, a_n, NT) + jnp.where(diag, var_ref[pl.ds(i_next, 1)], 0.0)
        s_ni = mm(t1_n, a_i, NT)
        aq = mm(a_i, q)
        linv, minv = factor_block(s_ref[...], jnp.sqrt(vcol_ref[i]))
        l_ni = mm(s_ni, linv, NT)
        s_ref[...] = s_nn - mm(l_ni, l_ni, NT)
        linv_ref[...] = linv
        minv_ref[...] = minv
        t1_ref[...] = t1
        aq_ref[...] = aq
        p_ref[...] = p
        qs_ref[i] = q
        qv_ref[...] = qv
        return carry

    lax.fori_loop(0, nb, step, 0)
    p, q, qv = finish_previous(nb)

    def over_obs(rows):
        total = jnp.zeros((8, members), F32)
        for i in range(nb):
            total = total + mm(jnp.broadcast_to(rows[i : i + 1], (8, B)), a_ref[i * B : (i + 1) * B])
        return total

    def times_a(v):
        return jnp.concatenate(
            [mm(v, a_ref[i * B : (i + 1) * B], NT)[0:1] for i in range(nb)], axis=0
        )

    d, var = d_ref[...], var_ref[...]
    w = (d - times_a(qv)) / var
    rest = d - var * w - times_a(over_obs(w))
    w = w + (rest - times_a(mm(over_obs(rest / var), p))) / var
    w_cols = columns_of(w)

    for i in range(nb):
        g = lz_ref[(i + 1) * B : (i + 2) * B]
        if i < nb - 1:
            inv = 1.0 / vcol_ref[i]
            g = g - mm(a_ref[i * B : (i + 1) * B], qs_ref[i + 1] - q) * jnp.concatenate([inv, inv], 1)
        gt_ref[:, i * B : (i + 1) * B] = g.T.astype(BF16)

    for lev in range(levels):
        damp_cols = columns_of(damp_ref[lev] * (1.0 / (members - 1.0)))
        slab = x_ref[lev]
        mean = jnp.zeros((8, cols), F32)
        for i in range(nb):
            f = mm16(yb_ref[i * B : (i + 1) * B], slab) * damp_cols[:, i : i + 1]
            k_ref[i * B : (i + 1) * B] = f.astype(BF16)
            mean = mean + jnp.sum((f * w_cols[:, i : i + 1]).reshape(B // 8, 8, cols), axis=0)
        xmo_ref[lev : lev + 1] = xm_ref[lev : lev + 1] + jnp.sum(mean, axis=0, keepdims=True)
        for half in range(cols // 256):
            lanes = slice(half * 256, (half + 1) * 256)
            inc = mm16(gt_ref[...], k_ref[:, lanes])
            xo_ref[lev, :, lanes] = (x_ref[lev, :, lanes].astype(F32) - inc).astype(BF16)


N_IN = 6


def first_kernel(*refs):
    ins, sites, outs, scratch = refs[:N_IN], refs[N_IN : N_IN + 4], refs[N_IN + 4 : N_IN + 7], refs[N_IN + 7 :]
    xo_ref, xmo_ref, share_ref = outs
    analyse(*ins, xo_ref, xmo_ref, *scratch)
    gather_sites(1, xo_ref, xmo_ref, *sites, share_ref)


def last_kernel(*refs):
    analyse(*refs)


def analysis_scratch(n, e, cols):
    nb = n // B

    def buf(*shape):
        return pltpu.VMEM(shape, F32)

    return [
        buf(n, e), pltpu.VMEM((n, e), BF16), buf(e, e), buf(nb + 1, e, e), buf(B, B), buf(B, B),
        buf(B, B), buf(B, e), buf(B, e), buf(8, e), buf(n + B, e), buf(nb + 1, 8, B), buf(nb, B),
        buf(nb, B, B), buf(nb, B), pltpu.VMEM((e, n), BF16), pltpu.VMEM((n, cols), BF16),
    ]


VMEM = pl.BlockSpec(memory_space=pltpu.VMEM)
PARAMS = pltpu.CompilerParams(vmem_limit_bytes=40 * 2**20)


def shards(
    perturb, mean_state, obs_value, obs_var, obs_weight, obs_tile, obs_col, obs_level,
    loc_horiz, loc_vert,
):
    levels, members, cols = perturb.shape
    batches, n = obs_tile.shape
    nb = n // B
    my_tile = lax.axis_index("horiz")
    first = lax.axis_index("lev") * levels
    near = lax.dynamic_slice_in_dim(loc_horiz, my_tile, 1, axis=1)
    damp = (near * lax.dynamic_slice_in_dim(loc_vert, first, levels, axis=1)).reshape(
        batches, levels, nb, B
    )
    sites = (obs_tile, obs_col, obs_level, obs_weight)
    values = obs_value.reshape(batches, nb, B)
    variances = obs_var.reshape(batches, nb, B)
    share_type = jax.ShapeDtypeStruct((2, 4, members // 8 + 1, 8, B), F32)
    state_types = (
        jax.ShapeDtypeStruct(perturb.shape, BF16),
        jax.ShapeDtypeStruct(mean_state.shape, F32),
    )
    scratch = analysis_scratch(n, members, cols)
    share = pl.pallas_call(
        gather_kernel, out_shape=share_type, in_specs=[VMEM] * 6, out_specs=VMEM,
        compiler_params=PARAMS, name="gather",
    )(perturb, mean_state, *sites)
    panel = sum_over_devices(share)
    perturb, mean_state, share = pl.pallas_call(
        first_kernel, out_shape=state_types + (share_type,), in_specs=[VMEM] * (N_IN + 4),
        out_specs=(VMEM,) * 3, scratch_shapes=scratch, compiler_params=PARAMS, name="analysis0",
    )(panel, perturb, mean_state, values[0], variances[0], damp[0], *sites)
    panel = sum_over_devices(share)
    return pl.pallas_call(
        last_kernel, out_shape=state_types, in_specs=[VMEM] * N_IN, out_specs=(VMEM,) * 2,
        scratch_shapes=scratch, compiler_params=PARAMS, name="analysis1",
    )(panel, perturb, mean_state, values[1], variances[1], damp[1])


def solution(mesh):
    return jax.shard_map(
        shards,
        mesh=mesh,
        in_specs=(P("lev", None, "horiz"), P("lev", "horiz")) + (P(),) * 8,
        out_specs=(P("lev", None, "horiz"), P("lev", "horiz")),
        check_vma=False,
    )
```

```python
import functools
import jax
import jax.numpy as jnp
from jax import lax
from jax.experimental import pallas as pl
from jax.experimental.pallas import tpu as pltpu
from jax.sharding import PartitionSpec as P

F32 = jnp.float32
BF16 = jnp.bfloat16
HIGHEST = lax.Precision.HIGHEST
MESH = pl.DeviceIdType.MESH
B = 128
Q = 32
NT = ((1,), (1,))
TN = ((0,), (0,))
NN = ((1,), (0,))


def mm(a, b, dims=NN):
    return lax.dot_general(a, b, (dims, ((), ())), precision=HIGHEST, preferred_element_type=F32)


def mm16(a, b):
    return jnp.dot(a, b, preferred_element_type=F32)


def columns_of(rows):
    return jnp.concatenate([rows] * 16, axis=0).T


def rows_at(i):
    return pl.ds(pl.multiple_of(i * B, B), B)


def in_three(rows):
    hi = rows.astype(BF16).astype(F32)
    mid = (rows - hi).astype(BF16).astype(F32)
    low = rows - hi - mid
    at = lax.broadcasted_iota(jnp.int32, (16, rows.shape[1]), 0)
    return jnp.where(at == 0, hi, jnp.where(at == 1, mid, jnp.where(at == 2, low, 0.0))).astype(BF16)


def one_hot(rows, index):
    at = lax.broadcasted_iota(jnp.int32, (rows, index.shape[1]), 0)
    return jnp.where(at == index, 1.0, 0.0)


def after(tile, col, cols, tiles):
    wraps = col == cols - 1
    next_tile = jnp.where(wraps, jnp.where(tile == tiles - 1, 0, tile + 1), tile)
    return wraps, next_tile, jnp.where(wraps, 0, col + 1)


def gather_sites(batch, across, x_ref, xm_ref, sites, out_ref):
    tile_ref, col_ref, level_ref, frac_ref = sites
    levels, members, cols = x_ref.shape
    tiles = lax.axis_size("horiz")
    my_tile = lax.axis_index("horiz")
    first = lax.axis_index("lev") * levels
    row = lax.broadcasted_iota(jnp.int32, (8, B), 0)
    width = 2 * B
    means = [in_three(xm_ref[lev : lev + 1, :]) for lev in range(levels)]
    for jb in range(4):
        lanes = slice(jb * width, (jb + 1) * width)
        tile, col, level, frac = (
            ref[batch : batch + 1, lanes] for ref in (tile_ref, col_ref, level_ref, frac_ref)
        )
        wraps, next_tile, next_col = after(tile, col, cols, tiles)
        if not across:
            next_col = jnp.where(wraps, -1, next_col)
        vals = []
        for t, c in ((tile, col), (next_tile, next_col)):
            v = jnp.zeros((members, width), F32)
            m = jnp.zeros((16, width), F32)
            for lev in range(levels):
                pos = jnp.where((t == my_tile) & (level == first + lev), c, -1)
                hot = one_hot(cols, pos).astype(BF16)
                v = v + mm16(x_ref[lev], hot)
                m = m + mm16(means[lev], hot)
            vals.append((v, jnp.sum(m[0:8], axis=0, keepdims=True)))
        site = (1.0 - frac) * vals[0][0] + frac * vals[1][0]
        mean = (1.0 - frac) * vals[0][1] + frac * vals[1][1]
        for core in range(2):
            half = slice(core * B, (core + 1) * B)
            out_ref[core, jb, 0:32] = site[:, half].reshape(32, 8, B)
            out_ref[core, jb, 32] = jnp.where(row == 0, mean[:, half], 0.0)


class Place:
    def __init__(self):
        horiz = lax.axis_index("horiz")
        lev = lax.axis_index("lev")
        self.x, self.z = horiz // 8, horiz % 8
        self.y, self.core = lev // 2, lev % 2
        self.other = 1 - self.core
        self.xs = [self.x] + [(self.x + k) % 4 for k in range(1, 4)]
        self.ys = [self.y] + [(self.y + k) % 4 for k in range(1, 4)]
        self.ys_back = [self.y] + [(self.y - k + 4) % 4 for k in range(1, 4)]
        self.zs = [self.z] + [(self.z + k) % 8 for k in range(1, 8)]
        self.to_core = (horiz, self.y * 2 + self.other)
        self.to_y = [None] + [(horiz, self.ys[k] * 2 + self.core) for k in range(1, 4)]
        self.to_x = [None] + [(self.xs[k] * 8 + self.z, lev) for k in range(1, 4)]
        self.to_z = [None] + [(self.x * 8 + self.zs[k], lev) for k in range(1, 8)]
        self.peers = [self.to_core] + self.to_y[1:] + self.to_x[1:] + self.to_z[1:]
        self.home = 8 * self.x + self.z
        self.x8 = 8 * self.x
        self.xs8 = [8 * v for v in self.xs]
        self.cell_home = 33 + self.home
        self.cell_x8 = 33 + self.x8


def sum_phases(place, c_ref, o_ref, bufs, send, recv, cells):
    r0, a0, r1, a1, r2, a2, r3 = bufs
    core, other, x, y, z = place.core, place.other, place.x, place.y, place.z
    sem = iter(range(COPIES))

    def copy(src, dst, peer):
        k = next(sem)
        return lambda: pltpu.make_async_remote_copy(
            src_ref=src, dst_ref=dst, send_sem=send.at[k], recv_sem=recv.at[k],
            device_id=peer, device_id_type=MESH,
        )

    order = (1, 2, 3, 0)
    to_core = [
        copy(c_ref.at[other, place.ys[k]], r0.at[place.ys[k]], place.to_core) for k in order
    ]
    to_y = [copy(a0.at[place.ys[k]], r1.at[k - 1], place.to_y[k]) for k in range(1, 4)]
    to_x, to_z, back_z, back_x = [], [], [], []
    for k in range(1, 4):
        to_x.append(copy(a1.at[pl.ds(place.xs8[k], 8)], r2.at[k - 1, pl.ds(0, 8)], place.to_x[k]))
        to_x.append(copy(a1.at[pl.ds(32, 1)], r2.at[k - 1, pl.ds(8, 1)], place.to_x[k]))
    for k in range(1, 8):
        to_z.append(copy(a2.at[pl.ds(place.zs[k], 1)], r3.at[k - 1, pl.ds(0, 1)], place.to_z[k]))
        to_z.append(copy(a2.at[pl.ds(8, 1)], r3.at[k - 1, pl.ds(1, 1)], place.to_z[k]))
    starts = (place.home, place.cell_home) if cells else (place.home,)
    for k in range(1, 8):
        for s in starts:
            spot = o_ref.at[core, y, pl.ds(s, 1)]
            back_z.append(copy(spot, spot, place.to_z[k]))
    starts = (place.x8, place.cell_x8) if cells else (place.x8,)
    for k in range(1, 4):
        for s in starts:
            spot = o_ref.at[core, y, pl.ds(s, 8)]
            back_x.append(copy(spot, spot, place.to_x[k]))
    spot = o_ref.at[core, y]
    back_y = [copy(spot, spot, place.to_y[k]) for k in range(1, 4)]
    back_core = []
    for k in range(4):
        spot = o_ref.at[core, place.ys_back[k]]
        back_core.append(copy(spot, spot, place.to_core))

    def start(copies):
        for c in copies:
            c().start()

    def arrive(copies):
        for c in copies:
            c().wait_recv()

    def begin():
        start(to_core)

    def add_core():
        for k, c in zip(order, to_core):
            c().wait_recv()
            yk = place.ys[k]
            a0[yk] = c_ref[core, yk] + r0[yk]
            if k:
                to_y[k - 1]().start()

    def add_y():
        arrive(to_y)
        a1[...] = (a0[y] + r1[0]) + (r1[1] + r1[2])
        start(to_x)

    def add_x():
        arrive(to_x)
        a2[0:8] = (a1[pl.ds(place.x8, 8)] + r2[0, 0:8]) + (r2[1, 0:8] + r2[2, 0:8])
        a2[8:9] = (a1[32:33] + r2[0, 8:9]) + (r2[1, 8:9] + r2[2, 8:9])
        start(to_z)

    def add_z():
        arrive(to_z)
        mine = a2[z]
        mean = a2[8]
        for k in range(7):
            mine = mine + r3[k, 0]
            mean = mean + r3[k, 1]
        o_ref[core, y, place.home] = mine
        o_ref[core, y, 32] = mean
        start(back_z)

    def return_x():
        arrive(back_z)
        start(back_x)

    def return_y():
        arrive(back_x)
        start(back_y)
        start(back_core[:1])

    def return_core():
        for k in range(3):
            back_y[k]().wait_recv()
            back_core[k + 1]().start()

    def end():
        arrive(back_core)
        for group in (to_core, to_y, to_x, to_z, back_z, back_x, back_y, back_core):
            for c in group:
                c().wait_send()

    return [begin, add_core, add_y, add_x, add_z, return_x, return_y, return_core, end]


COPIES = 4 + 3 + 6 + 14 + 14 + 6 + 3 + 4


def sum_buffers():
    def buf(*shape):
        return pltpu.VMEM(shape + (8, B), F32)

    return [buf(4, 33), buf(4, 33), buf(3, 33), buf(33), buf(3, 9), buf(9), buf(7, 2)]


def factor_block(s, dcol):
    nt = Q // 8
    row = lax.broadcasted_iota(jnp.int32, (8, B), 0)
    eye = jnp.where(
        lax.broadcasted_iota(jnp.int32, (B, B), 0) == lax.broadcasted_iota(jnp.int32, (B, B), 1),
        1.0,
        0.0,
    )
    m, a, z = s, eye, eye
    out_a, out_z = [], []
    for o in range(0, B, Q):
        w_t = [m[8 * t : 8 * t + 8] for t in range(nt)]
        a_t = [a[8 * t : 8 * t + 8] for t in range(nt)]
        z_t = [z[8 * t : 8 * t + 8] for t in range(nt)]
        cols = [
            [
                None if t < c // 8 else jnp.broadcast_to(w_t[t][:, o + c : o + c + 1], (8, B))
                for t in range(nt)
            ]
            for c in range(Q)
        ]
        for r in range(Q):
            tr, rr = r // 8, r % 8
            p = cols[r][tr][rr : rr + 1]
            rs = lax.rsqrt(p)
            l = [None if t < tr else cols[r][t] * rs for t in range(nt)]
            u = w_t[tr][rr : rr + 1] * rs
            av = a_t[tr][rr : rr + 1] * rs
            zv = z_t[tr][rr : rr + 1] / (p * rs + dcol[o + r : o + r + 1])
            for c in range(r + 1, Q):
                f = l[c // 8][c % 8 : c % 8 + 1]
                for t in range(c // 8, nt):
                    cols[c][t] = cols[c][t] - l[t] * f
            for t in range(tr, nt):
                lt = l[t] if t > tr else jnp.where(row > rr, l[t], 0.0)
                for rows, v in ((w_t, u), (a_t, av), (z_t, zv)):
                    new = rows[t] - lt * v
                    if t == tr:
                        new = jnp.where(row == rr, jnp.broadcast_to(v, (8, B)), new)
                    rows[t] = new
        u_b, a_b, z_b = (jnp.concatenate(rows, 0) for rows in (w_t, a_t, z_t))
        out_a.append(a_b)
        out_z.append(z_b)
        if o + Q < B:
            step = mm(u_b, jnp.concatenate([u_b, a_b, z_b], 1), TN)[o + Q :]
            m = m[Q:] - step[:, :B]
            a = a[Q:] - step[:, B : 2 * B]
            z = z[Q:] - step[:, 2 * B :]
    return jnp.concatenate(out_a, 0), jnp.concatenate(out_z, 0)


def rows8(ref, row):
    line = ref[row, :]
    return jnp.concatenate([line[:, k : k + B] for k in range(0, line.shape[1], B)], axis=0)


def analyse(site_of, mean_of, values, variances, damping, x_ref, xm_ref, hooks, between, scratch):
    (a_ref, yb_ref, p_ref, qs_ref, s_ref, linv_ref, minv_ref, t1_ref, aq_ref, qv_ref, lz_ref,
     d_ref, var_ref, vcol_ref, gt_ref, k_ref) = scratch
    levels, members, cols = x_ref.shape
    n = a_ref.shape[0]
    nb = n // B
    c = 1.0 / (members - 1.0) ** 0.5

    def square(k):
        return lax.broadcasted_iota(jnp.int32, (k, k), 0) == lax.broadcasted_iota(
            jnp.int32, (k, k), 1
        )

    eye_m = jnp.where(square(members), 1.0, 0.0)
    diag = square(B)
    for i in range(nb):
        y_i = site_of(i).T
        a_ref[i * B : (i + 1) * B] = y_i * c
        yb_ref[i * B : (i + 1) * B] = y_i.astype(BF16)
        d_ref[i : i + 1] = values[i : i + 1] - mean_of(i)
    var_ref[...] = variances
    var_cols = columns_of(variances)
    for i in range(nb):
        vcol_ref[i] = jnp.broadcast_to(var_cols[:, i : i + 1], (B, B))
    p_ref[...] = eye_m
    qs_ref[0] = eye_m * (1.0 / c)
    a_0 = a_ref[0:B]
    s_ref[...] = mm(a_0, a_0, NT) + jnp.where(diag, var_ref[0:1], 0.0)
    for ref in (linv_ref, minv_ref, t1_ref, aq_ref, qv_ref):
        ref[...] = jnp.zeros_like(ref)

    def finish_previous(i):
        linv, minv, t1 = linv_ref[...], minv_ref[...], t1_ref[...]
        ip = jnp.maximum(i - 1, 0)
        v = mm(linv, t1)
        z = mm(minv, aq_ref[...])
        lz_ref[rows_at(i)] = mm(linv, z, TN)
        p = p_ref[...] - mm(v, v, TN)
        q = qs_ref[ip] - mm(v, z, TN)
        qv = qv_ref[...]
        rhs = d_ref[pl.ds(ip, 1)] - mm(qv, a_ref[rows_at(ip)], NT)
        qv = qv + mm(mm(rhs, linv, NT), v)
        return p, q, qv

    def step(i, carry):
        p, q, qv = finish_previous(i)
        i_next = jnp.minimum(i + 1, nb - 1)
        a_i = a_ref[rows_at(i)]
        a_n = a_ref[rows_at(i_next)]
        t1 = mm(a_i, p)
        t1_n = mm(a_n, p)
        s_nn = mm(t1_n, a_n, NT) + jnp.where(diag, var_ref[pl.ds(i_next, 1)], 0.0)
        s_ni = mm(t1_n, a_i, NT)
        aq = mm(a_i, q)
        linv, minv = factor_block(s_ref[...], jnp.sqrt(vcol_ref[i]))
        l_ni = mm(s_ni, linv, NT)
        s_ref[...] = s_nn - mm(l_ni, l_ni, NT)
        linv_ref[...] = linv
        minv_ref[...] = minv
        t1_ref[...] = t1
        aq_ref[...] = aq
        p_ref[...] = p
        qs_ref[i] = q
        qv_ref[...] = qv
        for k, hook in enumerate(hooks):
            pl.when(i == k)(hook)
        return carry

    lax.fori_loop(0, nb, step, 0)
    p, q, qv = finish_previous(nb)

    def over_obs(rows):
        total = jnp.zeros((8, members), F32)
        for i in range(nb):
            total = total + mm(jnp.broadcast_to(rows[i : i + 1], (8, B)), a_ref[i * B : (i + 1) * B])
        return total

    def times_a(v):
        return jnp.concatenate(
            [mm(v, a_ref[i * B : (i + 1) * B], NT)[0:1] for i in range(nb)], axis=0
        )

    d, var = d_ref[...], var_ref[...]
    w = (d - times_a(qv)) / var
    rest = d - var * w - times_a(over_obs(w))
    w = w + (rest - times_a(mm(over_obs(rest / var), p))) / var
    w_cols = columns_of(w)

    for i in range(nb):
        g = lz_ref[(i + 1) * B : (i + 2) * B]
        if i < nb - 1:
            inv = 1.0 / vcol_ref[i]
            g = g - mm(a_ref[i * B : (i + 1) * B], qs_ref[i + 1] - q) * jnp.concatenate([inv, inv], 1)
        gt_ref[:, i * B : (i + 1) * B] = g.T.astype(BF16)

    w_lines = [w_cols[:, i : i + 1] for i in range(nb)]
    between(w_lines)
    for lev in range(levels):
        damp_cols = columns_of(damping[lev] * (1.0 / (members - 1.0)))
        slab = x_ref[lev]
        inc, mean = increments(
            lambda i: mm16(yb_ref[i * B : (i + 1) * B], slab) * damp_cols[:, i : i + 1],
            w_lines, gt_ref, k_ref,
        )
        xm_ref[lev : lev + 1] = xm_ref[lev : lev + 1] + mean
        x_ref[lev] = (slab.astype(F32) - inc).astype(BF16)


def increments(gain_of, w_lines, gt_ref, k_ref):
    mean = 0.0
    for i, w in enumerate(w_lines):
        f = gain_of(i)
        k_ref[i * B : (i + 1) * B] = f.astype(BF16)
        mean = mean + jnp.sum((f * w).reshape(B // 8, 8, f.shape[1]), axis=0)
    inc = [mm16(gt_ref[...], k_ref[:, c : c + 256]) for c in range(0, k_ref.shape[1], 256)]
    return jnp.concatenate(inc, axis=1), jnp.sum(mean, axis=0, keepdims=True)


def stack_three(rows):
    hi = rows.astype(BF16)
    mid = (rows - hi.astype(F32)).astype(BF16)
    low = (rows - hi.astype(F32) - mid.astype(F32)).astype(BF16)
    return jnp.concatenate([hi, mid, low], axis=0)


def pick_t(table, hot):
    return lax.dot_general(table, hot, (TN, ((), ())), preferred_element_type=F32)


def update_sites(share_ref, lh_ref, lv_ref, sites, scratch, w_lines, yt_ref, ym_ref, cells_ref):
    tile_ref, col_ref, level_ref, frac_ref = sites
    yb_ref, gt_ref, k_ref = scratch[1], scratch[14], scratch[15]
    n, members = yb_ref.shape
    cols = k_ref.shape[1]
    tiles, levels = lh_ref.shape[1], lv_ref.shape[1]
    lh = stack_three(lh_ref[0] * (1.0 / (members - 1.0)))
    lv = stack_three(lv_ref[0])

    def updated(slab, mean, tile, level):
        hi = slab.astype(BF16)
        low = (slab - hi.astype(F32)).astype(BF16)
        hot_t = one_hot(tiles, tile).astype(BF16)
        hot_l = one_hot(levels, level).astype(BF16)
        hot_t = jnp.concatenate([hot_t] * 3, axis=0)
        hot_l = jnp.concatenate([hot_l] * 3, axis=0)

        def gain_of(i):
            y_i = yb_ref[i * B : (i + 1) * B]
            damp = pick_t(lh[:, i * B : (i + 1) * B], hot_t) * pick_t(lv[:, i * B : (i + 1) * B], hot_l)
            return (mm16(y_i, hi) + mm16(y_i, low)) * damp

        inc, gained = increments(gain_of, w_lines, gt_ref, k_ref)
        return slab - inc, mean + gained

    at = lax.broadcasted_iota(jnp.int32, (8 * tiles, B), 0)
    cell = lax.broadcasted_iota(jnp.int32, (8 * tiles, B), 1)
    t_at, r_at = at // 8, at % 8
    top, bottom, middle = [], [], []
    for pair in range(4):
        parts = [0.0, 0.0, 0.0]
        for core in range(2):
            group = share_ref[core, pair, 33 : 33 + tiles].reshape(8 * tiles, B)
            c = cell - core * 2 * tiles
            lev_at = c // tiles
            hit = (c >= 0) & (c < 2 * tiles) & (c % tiles == t_at)
            for half in range(2):
                sel = jnp.where(hit & (r_at == 2 * lev_at + half), 1.0, 0.0).astype(BF16)
                parts[half] = parts[half] + pick_t(group.astype(BF16), sel)
            sel = jnp.where(hit & (r_at == 4 + lev_at), 1.0, 0.0)
            parts[2] = parts[2] + mm(group, sel, TN)[0:1]
        top.append(parts[0])
        bottom.append(parts[1])
        middle.append(parts[2])
    cells = jnp.concatenate([jnp.concatenate(top, 1), jnp.concatenate(bottom, 1)], 0)
    cell_mean = jnp.concatenate(middle, 1)
    index = lax.broadcasted_iota(jnp.int32, (1, cols), 1)
    cells, cell_mean = updated(cells, cell_mean, index % tiles, index // tiles)
    cells_ref[...] = cells.astype(BF16)
    cell_mean = in_three(cell_mean)
    for half in range(n // cols):
        lanes = slice(half * cols, (half + 1) * cols)
        tile, col, level, frac = (
            ref[1:2, lanes] for ref in (tile_ref, col_ref, level_ref, frac_ref)
        )
        spots = [(p % 2, p // 2) for p in range(4 * half, 4 * half + 4)]
        slab = jnp.concatenate([share_ref[c, y, 0:32].reshape(members, B) for c, y in spots], 1)
        mean = jnp.concatenate([share_ref[c, y, 32][0:1] for c, y in spots], 1)
        slab, mean = updated(slab, mean, tile, level)
        wraps, next_tile, _ = after(tile, col, cols, tiles)
        hot = one_hot(cols, jnp.where(wraps, level * tiles + next_tile, -1)).astype(BF16)
        yt_ref[:, lanes] = slab + frac * mm16(cells_ref[...], hot)
        ym_ref[0:1, lanes] = mean + frac * jnp.sum(mm16(cell_mean, hot)[0:8], axis=0, keepdims=True)


def whole_kernel(*refs):
    args, (x_ref, xm_ref), refs = refs[:10], refs[10:12], refs[12:]
    held, refs = refs[:8], refs[8:]
    share0, panel0, share1, panel1, refs = refs[0], refs[1], refs[2], refs[3], refs[4:]
    bufs0, bufs1, refs = refs[:7], refs[7:14], refs[14:]
    (load, send0, recv0, send1, recv1), refs = refs[:5], refs[5:]
    (yt_ref, ym_ref, cells_ref), scratch = refs[:3], refs[3:]

    barrier = pltpu.get_barrier_semaphore()
    place = Place()
    for peer in place.peers:
        pl.semaphore_signal(barrier, inc=1, device_id=peer, device_id_type=MESH)
    copies = [
        pltpu.make_async_copy(src, dst, load.at[k])
        for k, (src, dst) in enumerate(zip(args, (x_ref, xm_ref) + tuple(held)))
    ]
    for copy in copies:
        copy.start()
    for copy in copies:
        copy.wait()
    val_ref, var_ref, frac_ref, tile_ref, col_ref, level_ref, lh_ref, lv_ref = held
    sites = (tile_ref, col_ref, level_ref, frac_ref)
    levels, members, cols = x_ref.shape

    gather_sites(0, True, x_ref, xm_ref, sites, share0)
    pl.semaphore_wait(barrier, len(place.peers))
    first_sum = sum_phases(place, share0, panel0, bufs0, send0, recv0, False)
    second_sum = sum_phases(place, share1, panel1, bufs1, send1, recv1, True)
    first_sum[0]()
    gather_sites(1, False, x_ref, xm_ref, sites, share1)
    r16 = lax.broadcasted_iota(jnp.int32, (B, B), 0)
    own = jnp.zeros((8, B), F32)
    row = lax.broadcasted_iota(jnp.int32, (8, B), 0)
    for lev in range(levels):
        for half in range(2):
            block = x_ref[lev, half * B : (half + 1) * B, 0:B].astype(F32).T
            own = jnp.where(row == 2 * lev + half, block[0:1], own)
        own = jnp.where(row == 4 + lev, xm_ref[lev : lev + 1, 0:1], own)
    panel1[place.core, place.y, place.cell_home] = own
    for phase in first_sum[1:]:
        phase()
    second_sum[0]()

    def damping(batch):
        near = rows8(lh_ref.at[batch], pl.ds(place.home, 1))
        first = lax.axis_index("lev") * levels
        return [near * rows8(lv_ref.at[batch], pl.ds(first + lev, 1)) for lev in range(levels)]

    def between(w_lines):
        second_sum[8]()
        update_sites(panel1, lh_ref, lv_ref, sites, scratch, w_lines, yt_ref, ym_ref, cells_ref)

    hooks = second_sum[1:7] + [lambda: None, second_sum[7]]
    analyse(
        lambda i: panel0[i % 2, i // 2, 0:32].reshape(members, B),
        lambda i: panel0[i % 2, i // 2, 32][0:1],
        rows8(val_ref, slice(0, 1)), rows8(var_ref, slice(0, 1)), damping(0), x_ref, xm_ref,
        hooks, between, scratch,
    )
    analyse(
        lambda i: yt_ref[:, i * B : (i + 1) * B],
        lambda i: ym_ref[0:1, i * B : (i + 1) * B],
        rows8(val_ref, slice(1, 2)), rows8(var_ref, slice(1, 2)), damping(1), x_ref, xm_ref,
        [], lambda w_lines: None, scratch,
    )


def analysis_scratch(n, e, cols):
    nb = n // B

    def buf(*shape):
        return pltpu.VMEM(shape, F32)

    return [
        buf(n, e), pltpu.VMEM((n, e), BF16), buf(e, e), buf(nb + 1, e, e), buf(B, B), buf(B, B),
        buf(B, B), buf(B, e), buf(B, e), buf(8, e), buf(n + B, e), buf(nb, B), buf(nb, B),
        buf(nb, B, B), pltpu.VMEM((e, n), BF16), pltpu.VMEM((n, cols), BF16),
    ]


def shards(*args):
    perturb, mean_state, obs_value = args[:3]
    levels, members, cols = perturb.shape
    n = obs_value.shape[1]
    vm = pl.BlockSpec(memory_space=pltpu.VMEM)
    share = pltpu.VMEM((2, 4, members // 8 + 1, 8, B), F32)
    dma = pltpu.SemaphoreType.DMA
    return pl.pallas_call(
        whole_kernel,
        out_shape=(
            jax.ShapeDtypeStruct(perturb.shape, BF16),
            jax.ShapeDtypeStruct(mean_state.shape, F32),
        ),
        in_specs=[pl.BlockSpec(memory_space=pl.ANY)] * len(args),
        out_specs=(vm, vm),
        scratch_shapes=[pltpu.VMEM(a.shape, a.dtype) for a in args[2:]]
        + [share, share, share, pltpu.VMEM((2, 4, members // 8 + 33, 8, B), F32)]
        + sum_buffers()
        + sum_buffers()
        + [dma((len(args),))] + [dma((COPIES,))] * 4
        + [pltpu.VMEM((members, n), F32), pltpu.VMEM((8, n), F32), pltpu.VMEM((members, cols), BF16)]
        + analysis_scratch(n, members, cols),
        compiler_params=pltpu.CompilerParams(
            collective_id=0, has_side_effects=True, vmem_limit_bytes=48 * 2**20
        ),
        name="analysis",
    )(*args)


def solution(mesh):
    return jax.shard_map(
        shards,
        mesh=mesh,
        in_specs=(P("lev", None, "horiz"), P("lev", "horiz")) + (P(),) * 8,
        out_specs=(P("lev", None, "horiz"), P("lev", "horiz")),
        check_vma=False,
    )
```

```python
import functools
import jax
import jax.numpy as jnp
from jax import lax
from jax.experimental import pallas as pl
from jax.experimental.pallas import tpu as pltpu
from jax.sharding import PartitionSpec as P

F32 = jnp.float32
BF16 = jnp.bfloat16
HIGHEST = lax.Precision.HIGHEST
MESH = pl.DeviceIdType.MESH
B = 128
SUB = 16
Q = 64
NT = ((1,), (1,))
TN = ((0,), (0,))
NN = ((1,), (0,))


def mm(a, b, dims=NN):
    return lax.dot_general(a, b, (dims, ((), ())), precision=HIGHEST, preferred_element_type=F32)


def mm16(a, b):
    return jnp.dot(a, b, preferred_element_type=F32)


def columns_of(rows):
    return jnp.concatenate([rows] * 16, axis=0).T


def rows_at(i):
    return pl.ds(pl.multiple_of(i * B, B), B)


def in_three(rows):
    hi = rows.astype(BF16).astype(F32)
    mid = (rows - hi).astype(BF16).astype(F32)
    low = rows - hi - mid
    at = lax.broadcasted_iota(jnp.int32, (16, rows.shape[1]), 0)
    return jnp.where(at == 0, hi, jnp.where(at == 1, mid, jnp.where(at == 2, low, 0.0))).astype(BF16)


def one_hot(rows, index):
    at = lax.broadcasted_iota(jnp.int32, (rows, index.shape[1]), 0)
    return jnp.where(at == index, 1.0, 0.0)


def after(tile, col, cols, tiles):
    wraps = col == cols - 1
    next_tile = jnp.where(wraps, jnp.where(tile == tiles - 1, 0, tile + 1), tile)
    return wraps, next_tile, jnp.where(wraps, 0, col + 1)


def gather_sites(batch, across, x_ref, xm_ref, sites, out_ref):
    tile_ref, col_ref, level_ref, frac_ref = sites
    levels, members, cols = x_ref.shape
    tiles = lax.axis_size("horiz")
    my_tile = lax.axis_index("horiz")
    first = lax.axis_index("lev") * levels
    row = lax.broadcasted_iota(jnp.int32, (8, B), 0)
    width = 2 * B
    means = [in_three(xm_ref[lev : lev + 1, :]) for lev in range(levels)]
    for jb in range(4):
        lanes = slice(jb * width, (jb + 1) * width)
        tile, col, level, frac = (
            ref[batch : batch + 1, lanes] for ref in (tile_ref, col_ref, level_ref, frac_ref)
        )
        wraps, next_tile, next_col = after(tile, col, cols, tiles)
        if not across:
            next_col = jnp.where(wraps, -1, next_col)
        vals = []
        for t, c in ((tile, col), (next_tile, next_col)):
            v = jnp.zeros((members, width), F32)
            m = jnp.zeros((16, width), F32)
            for lev in range(levels):
                pos = jnp.where((t == my_tile) & (level == first + lev), c, -1)
                hot = one_hot(cols, pos).astype(BF16)
                v = v + mm16(x_ref[lev], hot)
                m = m + mm16(means[lev], hot)
            vals.append((v, jnp.sum(m[0:8], axis=0, keepdims=True)))
        site = (1.0 - frac) * vals[0][0] + frac * vals[1][0]
        mean = (1.0 - frac) * vals[0][1] + frac * vals[1][1]
        for core in range(2):
            half = slice(core * B, (core + 1) * B)
            out_ref[core, jb, 0:32] = site[:, half].reshape(32, 8, B)
            out_ref[core, jb, 32] = jnp.where(row == 0, mean[:, half], 0.0)


class Place:
    def __init__(self):
        horiz = lax.axis_index("horiz")
        lev = lax.axis_index("lev")
        self.x, self.z = horiz // 8, horiz % 8
        self.y, self.core = lev // 2, lev % 2
        self.other = 1 - self.core
        self.xs = [self.x] + [(self.x + k) % 4 for k in range(1, 4)]
        self.ys = [self.y] + [(self.y + k) % 4 for k in range(1, 4)]
        self.ys_back = [self.y] + [(self.y - k + 4) % 4 for k in range(1, 4)]
        self.zs = [self.z] + [(self.z + k) % 8 for k in range(1, 8)]
        self.to_core = (horiz, self.y * 2 + self.other)
        self.to_y = [None] + [(horiz, self.ys[k] * 2 + self.core) for k in range(1, 4)]
        self.to_x = [None] + [(self.xs[k] * 8 + self.z, lev) for k in range(1, 4)]
        self.to_z = [None] + [(self.x * 8 + self.zs[k], lev) for k in range(1, 8)]
        self.peers = [self.to_core] + self.to_y[1:] + self.to_x[1:] + self.to_z[1:]
        self.home = 8 * self.x + self.z
        self.x8 = 8 * self.x
        self.xs8 = [8 * v for v in self.xs]
        self.cell_home = 33 + self.home
        self.cell_x8 = 33 + self.x8


def sum_phases(place, c_ref, o_ref, bufs, send, recv, cells):
    r0, a0, r1, a1, r2, a2, r3 = bufs
    core, other, x, y, z = place.core, place.other, place.x, place.y, place.z
    sem = iter(range(COPIES))

    def copy(src, dst, peer):
        k = next(sem)
        return lambda: pltpu.make_async_remote_copy(
            src_ref=src, dst_ref=dst, send_sem=send.at[k], recv_sem=recv.at[k],
            device_id=peer, device_id_type=MESH,
        )

    order = (1, 2, 3, 0)
    to_core = [
        copy(c_ref.at[other, place.ys[k]], r0.at[place.ys[k]], place.to_core) for k in order
    ]
    to_y = [copy(a0.at[place.ys[k]], r1.at[k - 1], place.to_y[k]) for k in range(1, 4)]
    to_x, to_z, back_z, back_x = [], [], [], []
    for k in range(1, 4):
        to_x.append(copy(a1.at[pl.ds(place.xs8[k], 8)], r2.at[k - 1, pl.ds(0, 8)], place.to_x[k]))
        to_x.append(copy(a1.at[pl.ds(32, 1)], r2.at[k - 1, pl.ds(8, 1)], place.to_x[k]))
    for k in range(1, 8):
        to_z.append(copy(a2.at[pl.ds(place.zs[k], 1)], r3.at[k - 1, pl.ds(0, 1)], place.to_z[k]))
        to_z.append(copy(a2.at[pl.ds(8, 1)], r3.at[k - 1, pl.ds(1, 1)], place.to_z[k]))
    starts = (place.home, place.cell_home) if cells else (place.home,)
    for k in range(1, 8):
        for s in starts:
            spot = o_ref.at[core, y, pl.ds(s, 1)]
            back_z.append(copy(spot, spot, place.to_z[k]))
    starts = (place.x8, place.cell_x8) if cells else (place.x8,)
    for k in range(1, 4):
        for s in starts:
            spot = o_ref.at[core, y, pl.ds(s, 8)]
            back_x.append(copy(spot, spot, place.to_x[k]))
    spot = o_ref.at[core, y]
    back_y = [copy(spot, spot, place.to_y[k]) for k in range(1, 4)]
    back_core = []
    for k in range(4):
        spot = o_ref.at[core, place.ys_back[k]]
        back_core.append(copy(spot, spot, place.to_core))

    def start(copies):
        for c in copies:
            c().start()

    def arrive(copies):
        for c in copies:
            c().wait_recv()

    def begin():
        start(to_core)

    def add_core():
        for k, c in zip(order, to_core):
            c().wait_recv()
            yk = place.ys[k]
            a0[yk] = c_ref[core, yk] + r0[yk]
            if k:
                to_y[k - 1]().start()

    def add_y():
        arrive(to_y)
        a1[...] = (a0[y] + r1[0]) + (r1[1] + r1[2])
        start(to_x)

    def add_x():
        arrive(to_x)
        a2[0:8] = (a1[pl.ds(place.x8, 8)] + r2[0, 0:8]) + (r2[1, 0:8] + r2[2, 0:8])
        a2[8:9] = (a1[32:33] + r2[0, 8:9]) + (r2[1, 8:9] + r2[2, 8:9])
        start(to_z)

    def add_z():
        arrive(to_z)
        mine = a2[z]
        mean = a2[8]
        for k in range(7):
            mine = mine + r3[k, 0]
            mean = mean + r3[k, 1]
        o_ref[core, y, place.home] = mine
        o_ref[core, y, 32] = mean
        start(back_z)

    def return_x():
        arrive(back_z)
        start(back_x)

    def return_y():
        arrive(back_x)
        start(back_y)
        start(back_core[:1])

    def return_core():
        for k in range(3):
            back_y[k]().wait_recv()
            back_core[k + 1]().start()

    def end():
        arrive(back_core)
        for group in (to_core, to_y, to_x, to_z, back_z, back_x, back_y, back_core):
            for c in group:
                c().wait_send()

    return [begin, add_core, add_y, add_x, add_z, return_x, return_y, return_core, end]


COPIES = 4 + 3 + 6 + 14 + 14 + 6 + 3 + 4


def sum_buffers():
    def buf(*shape):
        return pltpu.VMEM(shape + (8, B), F32)

    return [buf(4, 33), buf(4, 33), buf(3, 33), buf(33), buf(3, 9), buf(9), buf(7, 2)]


def factor_block(s, dcol):
    nt = Q // 8
    row = lax.broadcasted_iota(jnp.int32, (8, B), 0)
    lane = lax.broadcasted_iota(jnp.int32, (8, B), 1)
    eye = jnp.where(
        lax.broadcasted_iota(jnp.int32, (B, B), 0) == lax.broadcasted_iota(jnp.int32, (B, B), 1),
        1.0,
        0.0,
    )
    both, shifted = s, eye
    out_a, out_z = [], []
    for o in range(0, B, Q):
        w_t = [both[8 * t : 8 * t + 8] for t in range(nt)]
        z_t = [shifted[8 * t : 8 * t + 8] for t in range(nt)]
        for sub in range(0, Q, SUB):
            begin, end = o + sub, o + sub + SUB
            own = (lane >= begin) & (lane < end)
            cols = {}
            for c in range(sub, sub + SUB):
                cols[c] = [
                    None if t < c // 8 else jnp.broadcast_to(w_t[t][:, o + c : o + c + 1], (8, B))
                    for t in range(nt)
                ]
            for t in range(sub // 8, nt):
                unit = lane == row + (o + 8 * t)
                if t < (sub + SUB) // 8:
                    w_t[t] = jnp.where(own, jnp.where(unit, 1.0, 0.0), w_t[t])
                else:
                    w_t[t] = jnp.where(own, 0.0, w_t[t])
            for r in range(sub, sub + SUB):
                tr, rr = r // 8, r % 8
                p = cols[r][tr][rr : rr + 1]
                rs = lax.rsqrt(p)
                l = [None if t < tr else cols[r][t] * rs for t in range(nt)]
                for c in range(r + 1, sub + SUB):
                    f = l[c // 8][c % 8 : c % 8 + 1]
                    for t in range(c // 8, nt):
                        cols[c][t] = cols[c][t] - l[t] * f
                scale = 1.0 / (p * rs + dcol[o + r : o + r + 1])
                for rows, v in ((w_t, w_t[tr][rr : rr + 1] * rs), (z_t, z_t[tr][rr : rr + 1] * scale)):
                    for t in range(tr, nt):
                        lt = l[t] if t > tr else jnp.where(row > rr, l[t], 0.0)
                        new = rows[t] - lt * v
                        if t == tr:
                            new = jnp.where(row == rr, jnp.broadcast_to(v, (8, B)), new)
                        rows[t] = new
            if sub + SUB < Q:
                ahead = (lane >= end) & (lane < o + Q)
                for t in range(sub // 8, (sub + SUB) // 8):
                    w_t[t] = jnp.where(ahead, 0.0, w_t[t])
        u_b, z_b = jnp.concatenate(w_t, 0), jnp.concatenate(z_t, 0)
        out_a.append(jnp.where(lax.broadcasted_iota(jnp.int32, (Q, B), 1) < o + Q, u_b, 0.0))
        out_z.append(z_b)
        if o + Q < B:
            step = mm(u_b, jnp.concatenate([u_b, z_b], 1), TN)[o + Q :]
            at = lax.broadcasted_iota(jnp.int32, (B - o - Q, B), 1)
            both = jnp.where((at >= o) & (at < o + Q), 0.0, both[Q:]) - step[:, :B]
            shifted = shifted[Q:] - step[:, B:]
    return jnp.concatenate(out_a, 0), jnp.concatenate(out_z, 0)


def rows8(ref, row):
    line = ref[row, :]
    return jnp.concatenate([line[:, k : k + B] for k in range(0, line.shape[1], B)], axis=0)


def analyse(site_of, mean_of, values, variances, damping, x_ref, xm_ref, hooks, between, scratch):
    (a_ref, yb_ref, p_ref, qs_ref, s_ref, linv_ref, minv_ref, t1_ref, aq_ref, qv_ref, lz_ref,
     d_ref, var_ref, vcol_ref, gt_ref, k_ref) = scratch
    levels, members, cols = x_ref.shape
    n = a_ref.shape[0]
    nb = n // B
    c = 1.0 / (members - 1.0) ** 0.5

    def square(k):
        return lax.broadcasted_iota(jnp.int32, (k, k), 0) == lax.broadcasted_iota(
            jnp.int32, (k, k), 1
        )

    eye_m = jnp.where(square(members), 1.0, 0.0)
    diag = square(B)
    for i in range(nb):
        y_i = site_of(i).T
        a_ref[i * B : (i + 1) * B] = y_i * c
        yb_ref[i * B : (i + 1) * B] = y_i.astype(BF16)
        d_ref[i : i + 1] = values[i : i + 1] - mean_of(i)
    var_ref[...] = variances
    var_cols = columns_of(variances)
    for i in range(nb):
        vcol_ref[i] = jnp.broadcast_to(var_cols[:, i : i + 1], (B, B))
    p_ref[...] = eye_m
    qs_ref[0] = eye_m * (1.0 / c)
    a_0 = a_ref[0:B]
    s_ref[...] = mm(a_0, a_0, NT) + jnp.where(diag, var_ref[0:1], 0.0)
    for ref in (linv_ref, minv_ref, t1_ref, aq_ref, qv_ref):
        ref[...] = jnp.zeros_like(ref)

    def finish_previous(i):
        linv, minv, t1 = linv_ref[...], minv_ref[...], t1_ref[...]
        ip = jnp.maximum(i - 1, 0)
        v = mm(linv, t1)
        z = mm(minv, aq_ref[...])
        lz_ref[rows_at(i)] = mm(linv, z, TN)
        p = p_ref[...] - mm(v, v, TN)
        q = qs_ref[ip] - mm(v, z, TN)
        qv = qv_ref[...]
        rhs = d_ref[pl.ds(ip, 1)] - mm(qv, a_ref[rows_at(ip)], NT)
        qv = qv + mm(mm(rhs, linv, NT), v)
        return p, q, qv

    def step(i, carry):
        p, q, qv = finish_previous(i)
        i_next = jnp.minimum(i + 1, nb - 1)
        a_i = a_ref[rows_at(i)]
        a_n = a_ref[rows_at(i_next)]
        t1 = mm(a_i, p)
        t1_n = mm(a_n, p)
        s_nn = mm(t1_n, a_n, NT) + jnp.where(diag, var_ref[pl.ds(i_next, 1)], 0.0)
        s_in = mm(a_i, t1_n, NT)
        aq = mm(a_i, q)
        linv, minv = factor_block(s_ref[...], jnp.sqrt(vcol_ref[i]))
        l_in = mm(linv, s_in)
        s_ref[...] = s_nn - mm(l_in, l_in, TN)
        linv_ref[...] = linv
        minv_ref[...] = minv
        t1_ref[...] = t1
        aq_ref[...] = aq
        p_ref[...] = p
        qs_ref[i] = q
        qv_ref[...] = qv
        for k, hook in enumerate(hooks):
            pl.when(i == k)(hook)
        return carry

    lax.fori_loop(0, nb, step, 0)
    p, q, qv = finish_previous(nb)

    def over_obs(rows):
        total = jnp.zeros((8, members), F32)
        for i in range(nb):
            total = total + mm(jnp.broadcast_to(rows[i : i + 1], (8, B)), a_ref[i * B : (i + 1) * B])
        return total

    def times_a(v):
        return jnp.concatenate(
            [mm(v, a_ref[i * B : (i + 1) * B], NT)[0:1] for i in range(nb)], axis=0
        )

    d, var = d_ref[...], var_ref[...]
    w = (d - times_a(qv)) / var
    rest = d - var * w - times_a(over_obs(w))
    w = w + (rest - times_a(mm(over_obs(rest / var), p))) / var
    w_cols = columns_of(w)

    for i in range(nb):
        g = lz_ref[(i + 1) * B : (i + 2) * B]
        if i < nb - 1:
            inv = 1.0 / vcol_ref[i]
            g = g - mm(a_ref[i * B : (i + 1) * B], qs_ref[i + 1] - q) * jnp.concatenate([inv, inv], 1)
        gt_ref[:, i * B : (i + 1) * B] = g.T.astype(BF16)

    w_lines = [w_cols[:, i : i + 1] for i in range(nb)]
    between(w_lines)
    for lev in range(levels):
        damp_cols = columns_of(damping[lev] * (1.0 / (members - 1.0)))
        slab = x_ref[lev]
        inc, mean = increments(
            lambda i: mm16(yb_ref[i * B : (i + 1) * B], slab) * damp_cols[:, i : i + 1],
            w_lines, gt_ref, k_ref,
        )
        xm_ref[lev : lev + 1] = xm_ref[lev : lev + 1] + mean
        x_ref[lev] = (slab.astype(F32) - inc).astype(BF16)


def increments(gain_of, w_lines, gt_ref, k_ref):
    mean = 0.0
    for i, w in enumerate(w_lines):
        f = gain_of(i)
        k_ref[i * B : (i + 1) * B] = f.astype(BF16)
        mean = mean + jnp.sum((f * w).reshape(B // 8, 8, f.shape[1]), axis=0)
    inc = [mm16(gt_ref[...], k_ref[:, c : c + 256]) for c in range(0, k_ref.shape[1], 256)]
    return jnp.concatenate(inc, axis=1), jnp.sum(mean, axis=0, keepdims=True)


def stack_three(rows):
    hi = rows.astype(BF16)
    mid = (rows - hi.astype(F32)).astype(BF16)
    low = (rows - hi.astype(F32) - mid.astype(F32)).astype(BF16)
    return jnp.concatenate([hi, mid, low], axis=0)


def pick_t(table, hot):
    return lax.dot_general(table, hot, (TN, ((), ())), preferred_element_type=F32)


def update_sites(share_ref, lh_ref, lv_ref, sites, scratch, w_lines, yt_ref, ym_ref, cells_ref):
    tile_ref, col_ref, level_ref, frac_ref = sites
    yb_ref, gt_ref, k_ref = scratch[1], scratch[14], scratch[15]
    n, members = yb_ref.shape
    cols = k_ref.shape[1]
    tiles, levels = lh_ref.shape[1], lv_ref.shape[1]
    lh = stack_three(lh_ref[0] * (1.0 / (members - 1.0)))
    lv = stack_three(lv_ref[0])

    def updated(slab, mean, tile, level):
        hi = slab.astype(BF16)
        low = (slab - hi.astype(F32)).astype(BF16)
        hot_t = one_hot(tiles, tile).astype(BF16)
        hot_l = one_hot(levels, level).astype(BF16)
        hot_t = jnp.concatenate([hot_t] * 3, axis=0)
        hot_l = jnp.concatenate([hot_l] * 3, axis=0)

        def gain_of(i):
            y_i = yb_ref[i * B : (i + 1) * B]
            damp = pick_t(lh[:, i * B : (i + 1) * B], hot_t) * pick_t(lv[:, i * B : (i + 1) * B], hot_l)
            return (mm16(y_i, hi) + mm16(y_i, low)) * damp

        inc, gained = increments(gain_of, w_lines, gt_ref, k_ref)
        return slab - inc, mean + gained

    at = lax.broadcasted_iota(jnp.int32, (8 * tiles, B), 0)
    cell = lax.broadcasted_iota(jnp.int32, (8 * tiles, B), 1)
    t_at, r_at = at // 8, at % 8
    top, bottom, middle = [], [], []
    for pair in range(4):
        parts = [0.0, 0.0, 0.0]
        for core in range(2):
            group = share_ref[core, pair, 33 : 33 + tiles].reshape(8 * tiles, B)
            c = cell - core * 2 * tiles
            lev_at = c // tiles
            hit = (c >= 0) & (c < 2 * tiles) & (c % tiles == t_at)
            for half in range(2):
                sel = jnp.where(hit & (r_at == 2 * lev_at + half), 1.0, 0.0).astype(BF16)
                parts[half] = parts[half] + pick_t(group.astype(BF16), sel)
            sel = jnp.where(hit & (r_at == 4 + lev_at), 1.0, 0.0)
            parts[2] = parts[2] + mm(group, sel, TN)[0:1]
        top.append(parts[0])
        bottom.append(parts[1])
        middle.append(parts[2])
    cells = jnp.concatenate([jnp.concatenate(top, 1), jnp.concatenate(bottom, 1)], 0)
    cell_mean = jnp.concatenate(middle, 1)
    index = lax.broadcasted_iota(jnp.int32, (1, cols), 1)
    cells, cell_mean = updated(cells, cell_mean, index % tiles, index // tiles)
    cells_ref[...] = cells.astype(BF16)
    cell_mean = in_three(cell_mean)
    for half in range(n // cols):
        lanes = slice(half * cols, (half + 1) * cols)
        tile, col, level, frac = (
            ref[1:2, lanes] for ref in (tile_ref, col_ref, level_ref, frac_ref)
        )
        spots = [(p % 2, p // 2) for p in range(4 * half, 4 * half + 4)]
        slab = jnp.concatenate([share_ref[c, y, 0:32].reshape(members, B) for c, y in spots], 1)
        mean = jnp.concatenate([share_ref[c, y, 32][0:1] for c, y in spots], 1)
        slab, mean = updated(slab, mean, tile, level)
        wraps, next_tile, _ = after(tile, col, cols, tiles)
        hot = one_hot(cols, jnp.where(wraps, level * tiles + next_tile, -1)).astype(BF16)
        yt_ref[:, lanes] = slab + frac * mm16(cells_ref[...], hot)
        ym_ref[0:1, lanes] = mean + frac * jnp.sum(mm16(cell_mean, hot)[0:8], axis=0, keepdims=True)


def whole_kernel(*refs):
    args, (x_ref, xm_ref), refs = refs[:10], refs[10:12], refs[12:]
    held, refs = refs[:8], refs[8:]
    share0, panel0, share1, panel1, refs = refs[0], refs[1], refs[2], refs[3], refs[4:]
    bufs0, bufs1, refs = refs[:7], refs[7:14], refs[14:]
    (load, send0, recv0, send1, recv1), refs = refs[:5], refs[5:]
    (yt_ref, ym_ref, cells_ref), scratch = refs[:3], refs[3:]

    barrier = pltpu.get_barrier_semaphore()
    place = Place()
    for peer in place.peers:
        pl.semaphore_signal(barrier, inc=1, device_id=peer, device_id_type=MESH)
    copies = [
        pltpu.make_async_copy(src, dst, load.at[k])
        for k, (src, dst) in enumerate(zip(args, (x_ref, xm_ref) + tuple(held)))
    ]
    for copy in copies:
        copy.start()
    for copy in copies:
        copy.wait()
    val_ref, var_ref, frac_ref, tile_ref, col_ref, level_ref, lh_ref, lv_ref = held
    sites = (tile_ref, col_ref, level_ref, frac_ref)
    levels, members, cols = x_ref.shape

    gather_sites(0, True, x_ref, xm_ref, sites, share0)
    pl.semaphore_wait(barrier, len(place.peers))
    first_sum = sum_phases(place, share0, panel0, bufs0, send0, recv0, False)
    second_sum = sum_phases(place, share1, panel1, bufs1, send1, recv1, True)
    first_sum[0]()
    gather_sites(1, False, x_ref, xm_ref, sites, share1)
    r16 = lax.broadcasted_iota(jnp.int32, (B, B), 0)
    own = jnp.zeros((8, B), F32)
    row = lax.broadcasted_iota(jnp.int32, (8, B), 0)
    for lev in range(levels):
        for half in range(2):
            block = x_ref[lev, half * B : (half + 1) * B, 0:B].astype(F32).T
            own = jnp.where(row == 2 * lev + half, block[0:1], own)
        own = jnp.where(row == 4 + lev, xm_ref[lev : lev + 1, 0:1], own)
    panel1[place.core, place.y, place.cell_home] = own
    for phase in first_sum[1:]:
        phase()
    second_sum[0]()

    def damping(batch):
        near = rows8(lh_ref.at[batch], pl.ds(place.home, 1))
        first = lax.axis_index("lev") * levels
        return [near * rows8(lv_ref.at[batch], pl.ds(first + lev, 1)) for lev in range(levels)]

    def between(w_lines):
        second_sum[8]()
        update_sites(panel1, lh_ref, lv_ref, sites, scratch, w_lines, yt_ref, ym_ref, cells_ref)

    hooks = second_sum[1:7] + [lambda: None, second_sum[7]]
    analyse(
        lambda i: panel0[i % 2, i // 2, 0:32].reshape(members, B),
        lambda i: panel0[i % 2, i // 2, 32][0:1],
        rows8(val_ref, slice(0, 1)), rows8(var_ref, slice(0, 1)), damping(0), x_ref, xm_ref,
        hooks, between, scratch,
    )
    analyse(
        lambda i: yt_ref[:, i * B : (i + 1) * B],
        lambda i: ym_ref[0:1, i * B : (i + 1) * B],
        rows8(val_ref, slice(1, 2)), rows8(var_ref, slice(1, 2)), damping(1), x_ref, xm_ref,
        [], lambda w_lines: None, scratch,
    )


def analysis_scratch(n, e, cols):
    nb = n // B

    def buf(*shape):
        return pltpu.VMEM(shape, F32)

    return [
        buf(n, e), pltpu.VMEM((n, e), BF16), buf(e, e), buf(nb + 1, e, e), buf(B, B), buf(B, B),
        buf(B, B), buf(B, e), buf(B, e), buf(8, e), buf(n + B, e), buf(nb, B), buf(nb, B),
        buf(nb, B, B), pltpu.VMEM((e, n), BF16), pltpu.VMEM((n, cols), BF16),
    ]


def shards(*args):
    perturb, mean_state, obs_value = args[:3]
    levels, members, cols = perturb.shape
    n = obs_value.shape[1]
    vm = pl.BlockSpec(memory_space=pltpu.VMEM)
    share = pltpu.VMEM((2, 4, members // 8 + 1, 8, B), F32)
    dma = pltpu.SemaphoreType.DMA
    return pl.pallas_call(
        whole_kernel,
        out_shape=(
            jax.ShapeDtypeStruct(perturb.shape, BF16),
            jax.ShapeDtypeStruct(mean_state.shape, F32),
        ),
        in_specs=[pl.BlockSpec(memory_space=pltpu.HBM)] * len(args),
        out_specs=(vm, vm),
        scratch_shapes=[pltpu.VMEM(a.shape, a.dtype) for a in args[2:]]
        + [share, share, share, pltpu.VMEM((2, 4, members // 8 + 33, 8, B), F32)]
        + sum_buffers()
        + sum_buffers()
        + [dma((len(args),))] + [dma((COPIES,))] * 4
        + [pltpu.VMEM((members, n), F32), pltpu.VMEM((8, n), F32), pltpu.VMEM((members, cols), BF16)]
        + analysis_scratch(n, members, cols),
        compiler_params=pltpu.CompilerParams(
            collective_id=0, has_side_effects=True, vmem_limit_bytes=60 * 2**20
        ),
        name="analysis",
    )(*args)


def solution(mesh):
    return jax.shard_map(
        shards,
        mesh=mesh,
        in_specs=(P("lev", None, "horiz"), P("lev", "horiz")) + (P(),) * 8,
        out_specs=(P("lev", None, "horiz"), P("lev", "horiz")),
        check_vma=False,
    )
```

```python
import functools
import jax
import jax.numpy as jnp
from jax import lax
from jax.experimental import pallas as pl
from jax.experimental.pallas import tpu as pltpu
from jax.sharding import PartitionSpec as P

F32 = jnp.float32
BF16 = jnp.bfloat16
HIGHEST = lax.Precision.HIGHEST
MESH = pl.DeviceIdType.MESH
B = 128
SUB = 16
Q = 64
NT = ((1,), (1,))
TN = ((0,), (0,))
NN = ((1,), (0,))


def mm(a, b, dims=NN):
    return lax.dot_general(a, b, (dims, ((), ())), precision=HIGHEST, preferred_element_type=F32)


def mm16(a, b):
    return jnp.dot(a, b, preferred_element_type=F32)


def columns_of(rows):
    return jnp.concatenate([rows] * 16, axis=0).T


def rows_at(i):
    return pl.ds(pl.multiple_of(i * B, B), B)


def in_three(rows):
    hi = rows.astype(BF16).astype(F32)
    mid = (rows - hi).astype(BF16).astype(F32)
    low = rows - hi - mid
    at = lax.broadcasted_iota(jnp.int32, (16, rows.shape[1]), 0)
    return jnp.where(at == 0, hi, jnp.where(at == 1, mid, jnp.where(at == 2, low, 0.0))).astype(BF16)


def one_hot(rows, index):
    at = lax.broadcasted_iota(jnp.int32, (rows, index.shape[1]), 0)
    return jnp.where(at == index, 1.0, 0.0)


def after(tile, col, cols, tiles):
    wraps = col == cols - 1
    next_tile = jnp.where(wraps, jnp.where(tile == tiles - 1, 0, tile + 1), tile)
    return wraps, next_tile, jnp.where(wraps, 0, col + 1)


def gather_sites(batch, across, quarters, x_ref, xm_ref, sites, put):
    tile_ref, col_ref, level_ref, frac_ref = sites
    levels, members, cols = x_ref.shape
    tiles = lax.axis_size("horiz")
    my_tile = lax.axis_index("horiz")
    first = lax.axis_index("lev") * levels
    row = lax.broadcasted_iota(jnp.int32, (8, B), 0)
    width = 2 * B
    means = [in_three(xm_ref[lev : lev + 1, :]) for lev in range(levels)]
    for jb in quarters:
        lanes = slice(jb * width, (jb + 1) * width)
        tile, col, level, frac = (
            ref[batch : batch + 1, lanes] for ref in (tile_ref, col_ref, level_ref, frac_ref)
        )
        wraps, next_tile, next_col = after(tile, col, cols, tiles)
        if not across:
            next_col = jnp.where(wraps, -1, next_col)
        vals = []
        for t, c in ((tile, col), (next_tile, next_col)):
            v = jnp.zeros((members, width), F32)
            m = jnp.zeros((16, width), F32)
            for lev in range(levels):
                pos = jnp.where((t == my_tile) & (level == first + lev), c, -1)
                hot = one_hot(cols, pos).astype(BF16)
                v = v + mm16(x_ref[lev], hot)
                m = m + mm16(means[lev], hot)
            vals.append((v, jnp.sum(m[0:8], axis=0, keepdims=True)))
        site = (1.0 - frac) * vals[0][0] + frac * vals[1][0]
        mean = (1.0 - frac) * vals[0][1] + frac * vals[1][1]
        for core in range(2):
            half = slice(core * B, (core + 1) * B)
            put(2 * jb + core, site[:, half], jnp.where(row == 0, mean[:, half], 0.0))


class Place:
    def __init__(self):
        horiz = lax.axis_index("horiz")
        lev = lax.axis_index("lev")
        self.x, self.z = horiz // 8, horiz % 8
        self.y, self.core = lev // 2, lev % 2
        self.other = 1 - self.core
        self.xs = [self.x] + [(self.x + k) % 4 for k in range(1, 4)]
        self.ys = [self.y] + [(self.y + k) % 4 for k in range(1, 4)]
        self.ys_back = [self.y] + [(self.y - k + 4) % 4 for k in range(1, 4)]
        self.zs = [self.z] + [(self.z + k) % 8 for k in range(1, 8)]
        self.to_core = (horiz, self.y * 2 + self.other)
        self.to_y = [None] + [(horiz, self.ys[k] * 2 + self.core) for k in range(1, 4)]
        self.to_x = [None] + [(self.xs[k] * 8 + self.z, lev) for k in range(1, 4)]
        self.to_z = [None] + [(self.x * 8 + self.zs[k], lev) for k in range(1, 8)]
        self.peers = [self.to_core] + self.to_y[1:] + self.to_x[1:] + self.to_z[1:]
        self.home = 8 * self.x + self.z
        self.x8 = 8 * self.x
        self.xs8 = [8 * v for v in self.xs]
        self.cell_home = 33 + self.home
        self.cell_x8 = 33 + self.x8
        self.zs2 = [2 * v for v in self.zs]


def sum_phases(place, c_ref, o_ref, bufs, send, recv, cells):
    r0, a0, r1, a1, r2, a2, r3 = bufs
    core, other, x, y, z = place.core, place.other, place.x, place.y, place.z
    sem = iter(range(COPIES))

    def copy(src, dst, peer):
        k = next(sem)
        return lambda: pltpu.make_async_remote_copy(
            src_ref=src, dst_ref=dst, send_sem=send.at[k], recv_sem=recv.at[k],
            device_id=peer, device_id_type=MESH,
        )

    order = (1, 2, 3, 0)
    to_core = [
        copy(c_ref.at[other, place.ys[k]], r0.at[place.ys[k]], place.to_core) for k in order
    ]
    to_y = [copy(a0.at[place.ys[k]], r1.at[k - 1], place.to_y[k]) for k in range(1, 4)]
    to_x, to_z, back_z, back_x = [], [], [], []
    for k in range(1, 4):
        to_x.append(copy(a1.at[pl.ds(place.xs8[k], 8)], r2.at[k - 1, pl.ds(0, 8)], place.to_x[k]))
        to_x.append(copy(a1.at[pl.ds(32, 1)], r2.at[k - 1, pl.ds(8, 1)], place.to_x[k]))
    for k in range(1, 8):
        to_z.append(copy(a2.at[pl.ds(place.zs[k], 1)], r3.at[k - 1, pl.ds(0, 1)], place.to_z[k]))
        to_z.append(copy(a2.at[pl.ds(8, 1)], r3.at[k - 1, pl.ds(1, 1)], place.to_z[k]))
    starts = (place.home, place.cell_home) if cells else (place.home,)
    for k in range(1, 8):
        for s in starts:
            spot = o_ref.at[core, y, pl.ds(s, 1)]
            back_z.append(copy(spot, spot, place.to_z[k]))
    starts = (place.x8, place.cell_x8) if cells else (place.x8,)
    for k in range(1, 4):
        for s in starts:
            spot = o_ref.at[core, y, pl.ds(s, 8)]
            back_x.append(copy(spot, spot, place.to_x[k]))
    spot = o_ref.at[core, y]
    back_y = [copy(spot, spot, place.to_y[k]) for k in range(1, 4)]
    back_core = []
    for k in range(4):
        spot = o_ref.at[core, place.ys_back[k]]
        back_core.append(copy(spot, spot, place.to_core))

    def start(copies):
        for c in copies:
            c().start()

    def arrive(copies):
        for c in copies:
            c().wait_recv()

    def begin():
        start(to_core)

    def add_core():
        for k, c in zip(order, to_core):
            c().wait_recv()
            yk = place.ys[k]
            a0[yk] = c_ref[core, yk] + r0[yk]
            if k:
                to_y[k - 1]().start()

    def add_y():
        arrive(to_y)
        a1[...] = (a0[y] + r1[0]) + (r1[1] + r1[2])
        start(to_x)

    def add_x():
        arrive(to_x)
        a2[0:8] = (a1[pl.ds(place.x8, 8)] + r2[0, 0:8]) + (r2[1, 0:8] + r2[2, 0:8])
        a2[8:9] = (a1[32:33] + r2[0, 8:9]) + (r2[1, 8:9] + r2[2, 8:9])
        start(to_z)

    def add_z():
        arrive(to_z)
        mine = a2[z]
        mean = a2[8]
        for k in range(7):
            mine = mine + r3[k, 0]
            mean = mean + r3[k, 1]
        o_ref[core, y, place.home] = mine
        o_ref[core, y, 32] = mean
        start(back_z)

    def return_x():
        arrive(back_z)
        start(back_x)

    def return_y():
        arrive(back_x)
        start(back_y)
        start(back_core[:1])

    def return_core():
        for k in range(3):
            back_y[k]().wait_recv()
            back_core[k + 1]().start()

    def end():
        arrive(back_core)
        for group in (to_core, to_y, to_x, to_z, back_z, back_x, back_y, back_core):
            for c in group:
                c().wait_send()

    return [begin, add_core, add_y, add_x, add_z, return_x, return_y, return_core, end]


def half_sum_phases(place, c_ref, o_ref, bufs, send, recv):
    r0, a0, r1, a1, r2, a2, r3 = bufs
    core, other, y = place.core, place.other, place.y
    sem = iter(range(COPIES))

    def copy(src, dst, peer):
        k = next(sem)
        return lambda: pltpu.make_async_remote_copy(
            src_ref=src, dst_ref=dst, send_sem=send.at[k], recv_sem=recv.at[k],
            device_id=peer, device_id_type=MESH,
        )

    order = (1, 2, 3, 0)
    to_core = [
        copy(c_ref.at[other, place.ys[k]], r0.at[place.ys[k]], place.to_core) for k in order
    ]
    to_y = [copy(a0.at[place.ys[k]], r1.at[k - 1], place.to_y[k]) for k in range(1, 4)]
    to_z, back_z = [], []
    for k in range(1, 8):
        to_z.append(copy(a1.at[pl.ds(place.zs2[k], 2)], r2.at[k - 1, pl.ds(0, 2)], place.to_z[k]))
        to_z.append(copy(a1.at[pl.ds(16, 1)], r2.at[k - 1, pl.ds(2, 1)], place.to_z[k]))
    to_x = [copy(a2, r3.at[k - 1], place.to_x[k]) for k in range(1, 4)]
    for k in range(1, 8):
        spot = o_ref.at[core, y, pl.ds(place.zs2[0], 2)]
        back_z.append(copy(spot, spot, place.to_z[k]))
    spot = o_ref.at[core, y]
    back_y = [copy(spot, spot, place.to_y[k]) for k in range(1, 4)]
    back_core = []
    for k in range(4):
        spot = o_ref.at[core, place.ys_back[k]]
        back_core.append(copy(spot, spot, place.to_core))

    def start(copies):
        for c in copies:
            c().start()

    def arrive(copies):
        for c in copies:
            c().wait_recv()

    def begin():
        start(to_core)

    def add_core():
        for k, c in zip(order, to_core):
            c().wait_recv()
            yk = place.ys[k]
            a0[yk] = c_ref[core, yk] + r0[yk]
            if k:
                to_y[k - 1]().start()

    def add_y():
        arrive(to_y)
        a1[...] = (a0[y] + r1[0]) + (r1[1] + r1[2])
        start(to_z)

    def add_z():
        arrive(to_z)
        mine = a1[pl.ds(place.zs2[0], 2)]
        mean = a1[16:17]
        for k in range(7):
            mine = mine + r2[k, 0:2]
            mean = mean + r2[k, 2:3]
        a2[0:2] = mine
        a2[2:3] = mean
        start(to_x)

    def add_x():
        arrive(to_x)
        total = (a2[...] + r3[0]) + (r3[1] + r3[2])
        o_ref[core, y, pl.ds(place.zs2[0], 2)] = total[0:2]
        o_ref[core, y, 16] = total[2]
        start(back_z)

    def return_y():
        arrive(back_z)
        start(back_y)
        start(back_core[:1])

    def return_core():
        for k in range(3):
            back_y[k]().wait_recv()
            back_core[k + 1]().start()

    def end():
        arrive(back_core)
        for group in (to_core, to_y, to_z, to_x, back_z, back_y, back_core):
            for c in group:
                c().wait_send()

    return [begin, add_core, add_y, add_z, add_x, return_y, return_core, end]


COPIES = 4 + 3 + 6 + 14 + 14 + 6 + 3 + 4


def sum_buffers():
    def buf(*shape):
        return pltpu.VMEM(shape + (8, B), F32)

    return [buf(4, 33), buf(4, 33), buf(3, 33), buf(33), buf(3, 9), buf(9), buf(7, 2)]


def half_sum_buffers():
    def buf(*shape):
        return pltpu.VMEM(shape + (8, B), F32)

    return [buf(4, 17), buf(4, 17), buf(3, 17), buf(17), buf(7, 3), buf(3), buf(3, 3)]


def factor_block(s, dcol):
    nt = Q // 8
    row = lax.broadcasted_iota(jnp.int32, (8, B), 0)
    lane = lax.broadcasted_iota(jnp.int32, (8, B), 1)
    eye = jnp.where(
        lax.broadcasted_iota(jnp.int32, (B, B), 0) == lax.broadcasted_iota(jnp.int32, (B, B), 1),
        1.0,
        0.0,
    )
    both, shifted = s, eye
    out_a, out_z = [], []
    for o in range(0, B, Q):
        w_t = [both[8 * t : 8 * t + 8] for t in range(nt)]
        z_t = [shifted[8 * t : 8 * t + 8] for t in range(nt)]
        for sub in range(0, Q, SUB):
            begin, end = o + sub, o + sub + SUB
            own = (lane >= begin) & (lane < end)
            cols = {}
            for c in range(sub, sub + SUB):
                cols[c] = [
                    None if t < c // 8 else jnp.broadcast_to(w_t[t][:, o + c : o + c + 1], (8, B))
                    for t in range(nt)
                ]
            for t in range(sub // 8, nt):
                unit = lane == row + (o + 8 * t)
                if t < (sub + SUB) // 8:
                    w_t[t] = jnp.where(own, jnp.where(unit, 1.0, 0.0), w_t[t])
                else:
                    w_t[t] = jnp.where(own, 0.0, w_t[t])
            for r in range(sub, sub + SUB):
                tr, rr = r // 8, r % 8
                p = cols[r][tr][rr : rr + 1]
                rs = lax.rsqrt(p)
                l = [None if t < tr else cols[r][t] * rs for t in range(nt)]
                for c in range(r + 1, sub + SUB):
                    f = l[c // 8][c % 8 : c % 8 + 1]
                    for t in range(c // 8, nt):
                        cols[c][t] = cols[c][t] - l[t] * f
                scale = 1.0 / (p * rs + dcol[o + r : o + r + 1])
                for rows, v in ((w_t, w_t[tr][rr : rr + 1] * rs), (z_t, z_t[tr][rr : rr + 1] * scale)):
                    for t in range(tr, nt):
                        lt = l[t] if t > tr else jnp.where(row > rr, l[t], 0.0)
                        new = rows[t] - lt * v
                        if t == tr:
                            new = jnp.where(row == rr, jnp.broadcast_to(v, (8, B)), new)
                        rows[t] = new
            if sub + SUB < Q:
                ahead = (lane >= end) & (lane < o + Q)
                for t in range(sub // 8, (sub + SUB) // 8):
                    w_t[t] = jnp.where(ahead, 0.0, w_t[t])
        u_b, z_b = jnp.concatenate(w_t, 0), jnp.concatenate(z_t, 0)
        out_a.append(jnp.where(lax.broadcasted_iota(jnp.int32, (Q, B), 1) < o + Q, u_b, 0.0))
        out_z.append(z_b)
        if o + Q < B:
            step = mm(u_b, jnp.concatenate([u_b, z_b], 1), TN)[o + Q :]
            at = lax.broadcasted_iota(jnp.int32, (B - o - Q, B), 1)
            both = jnp.where((at >= o) & (at < o + Q), 0.0, both[Q:]) - step[:, :B]
            shifted = shifted[Q:] - step[:, B:]
    return jnp.concatenate(out_a, 0), jnp.concatenate(out_z, 0)


def rows8(ref, row):
    line = ref[row, :]
    return jnp.concatenate([line[:, k : k + B] for k in range(0, line.shape[1], B)], axis=0)


def analyse(site_of, mean_of, values, variances, damping, x_ref, xm_ref, hooks, between, scratch,
            late):
    (a_ref, yb_ref, p_ref, qs_ref, s_ref, linv_ref, minv_ref, t1_ref, aq_ref, qv_ref, lz_ref,
     d_ref, var_ref, vcol_ref, gt_ref, k_ref) = scratch
    levels, members, cols = x_ref.shape
    n = a_ref.shape[0]
    nb = n // B
    c = 1.0 / (members - 1.0) ** 0.5

    def square(k):
        return lax.broadcasted_iota(jnp.int32, (k, k), 0) == lax.broadcasted_iota(
            jnp.int32, (k, k), 1
        )

    eye_m = jnp.where(square(members), 1.0, 0.0)
    diag = square(B)
    def fill(blocks):
        for i in blocks:
            y_i = site_of(i).T
            a_ref[i * B : (i + 1) * B] = y_i * c
            yb_ref[i * B : (i + 1) * B] = y_i.astype(BF16)
            d_ref[i : i + 1] = values[i : i + 1] - mean_of(i)

    fill(range(nb - late))
    var_ref[...] = variances
    var_cols = columns_of(variances)
    for i in range(nb):
        vcol_ref[i] = jnp.broadcast_to(var_cols[:, i : i + 1], (B, B))
    p_ref[...] = eye_m
    qs_ref[0] = eye_m * (1.0 / c)
    a_0 = a_ref[0:B]
    s_ref[...] = mm(a_0, a_0, NT) + jnp.where(diag, var_ref[0:1], 0.0)
    for ref in (linv_ref, minv_ref, t1_ref, aq_ref, qv_ref):
        ref[...] = jnp.zeros_like(ref)

    def finish_previous(i):
        linv, minv, t1 = linv_ref[...], minv_ref[...], t1_ref[...]
        ip = jnp.maximum(i - 1, 0)
        v = mm(linv, t1)
        z = mm(minv, aq_ref[...])
        lz_ref[rows_at(i)] = mm(linv, z, TN)
        p = p_ref[...] - mm(v, v, TN)
        q = qs_ref[ip] - mm(v, z, TN)
        qv = qv_ref[...]
        rhs = d_ref[pl.ds(ip, 1)] - mm(qv, a_ref[rows_at(ip)], NT)
        qv = qv + mm(mm(rhs, linv, NT), v)
        return p, q, qv

    def step(i, carry):
        p, q, qv = finish_previous(i)
        i_next = jnp.minimum(i + 1, nb - 1)
        a_i = a_ref[rows_at(i)]
        a_n = a_ref[rows_at(i_next)]
        t1 = mm(a_i, p)
        t1_n = mm(a_n, p)
        s_nn = mm(t1_n, a_n, NT) + jnp.where(diag, var_ref[pl.ds(i_next, 1)], 0.0)
        s_in = mm(a_i, t1_n, NT)
        aq = mm(a_i, q)
        linv, minv = factor_block(s_ref[...], jnp.sqrt(vcol_ref[i]))
        l_in = mm(linv, s_in)
        s_ref[...] = s_nn - mm(l_in, l_in, TN)
        linv_ref[...] = linv
        minv_ref[...] = minv
        t1_ref[...] = t1
        aq_ref[...] = aq
        p_ref[...] = p
        qs_ref[i] = q
        qv_ref[...] = qv
        for k, hook in enumerate(hooks):
            pl.when(i == k)(hook)
        if late:
            pl.when(i == nb - late - 2)(lambda: fill(range(nb - late, nb)))
        return carry

    lax.fori_loop(0, nb, step, 0)
    p, q, qv = finish_previous(nb)

    def over_obs(rows):
        total = jnp.zeros((8, members), F32)
        for i in range(nb):
            total = total + mm(jnp.broadcast_to(rows[i : i + 1], (8, B)), a_ref[i * B : (i + 1) * B])
        return total

    def times_a(v):
        return jnp.concatenate(
            [mm(v, a_ref[i * B : (i + 1) * B], NT)[0:1] for i in range(nb)], axis=0
        )

    d, var = d_ref[...], var_ref[...]
    w = (d - times_a(qv)) / var
    rest = d - var * w - times_a(over_obs(w))
    w = w + (rest - times_a(mm(over_obs(rest / var), p))) / var
    w_cols = columns_of(w)

    for i in range(nb):
        g = lz_ref[(i + 1) * B : (i + 2) * B]
        if i < nb - 1:
            inv = 1.0 / vcol_ref[i]
            g = g - mm(a_ref[i * B : (i + 1) * B], qs_ref[i + 1] - q) * jnp.concatenate([inv, inv], 1)
        gt_ref[:, i * B : (i + 1) * B] = g.T.astype(BF16)

    w_lines = [w_cols[:, i : i + 1] for i in range(nb)]
    between(w_lines)
    for lev in range(levels):
        damp_cols = columns_of(damping[lev] * (1.0 / (members - 1.0)))
        slab = x_ref[lev]
        inc, mean = increments(
            lambda i: mm16(yb_ref[i * B : (i + 1) * B], slab) * damp_cols[:, i : i + 1],
            w_lines, gt_ref, k_ref,
        )
        xm_ref[lev : lev + 1] = xm_ref[lev : lev + 1] + mean
        x_ref[lev] = (slab.astype(F32) - inc).astype(BF16)


def increments(gain_of, w_lines, gt_ref, k_ref):
    mean = 0.0
    for i, w in enumerate(w_lines):
        f = gain_of(i)
        k_ref[i * B : (i + 1) * B] = f.astype(BF16)
        mean = mean + jnp.sum((f * w).reshape(B // 8, 8, f.shape[1]), axis=0)
    inc = [mm16(gt_ref[...], k_ref[:, c : c + 256]) for c in range(0, k_ref.shape[1], 256)]
    return jnp.concatenate(inc, axis=1), jnp.sum(mean, axis=0, keepdims=True)


def stack_three(rows):
    hi = rows.astype(BF16)
    mid = (rows - hi.astype(F32)).astype(BF16)
    low = (rows - hi.astype(F32) - mid.astype(F32)).astype(BF16)
    return jnp.concatenate([hi, mid, low], axis=0)


def pick_t(table, hot):
    return lax.dot_general(table, hot, (TN, ((), ())), preferred_element_type=F32)


def update_sites(share_ref, lh_ref, lv_ref, sites, scratch, w_lines, yt_ref, ym_ref, cells_ref):
    tile_ref, col_ref, level_ref, frac_ref = sites
    yb_ref, gt_ref, k_ref = scratch[1], scratch[14], scratch[15]
    n, members = yb_ref.shape
    cols = k_ref.shape[1]
    tiles, levels = lh_ref.shape[1], lv_ref.shape[1]
    lh = stack_three(lh_ref[0] * (1.0 / (members - 1.0)))
    lv = stack_three(lv_ref[0])

    def updated(slab, mean, tile, level):
        hi = slab.astype(BF16)
        low = (slab - hi.astype(F32)).astype(BF16)
        hot_t = one_hot(tiles, tile).astype(BF16)
        hot_l = one_hot(levels, level).astype(BF16)
        hot_t = jnp.concatenate([hot_t] * 3, axis=0)
        hot_l = jnp.concatenate([hot_l] * 3, axis=0)

        def gain_of(i):
            y_i = yb_ref[i * B : (i + 1) * B]
            damp = pick_t(lh[:, i * B : (i + 1) * B], hot_t) * pick_t(lv[:, i * B : (i + 1) * B], hot_l)
            return (mm16(y_i, hi) + mm16(y_i, low)) * damp

        inc, gained = increments(gain_of, w_lines, gt_ref, k_ref)
        return slab - inc, mean + gained

    at = lax.broadcasted_iota(jnp.int32, (8 * tiles, B), 0)
    cell = lax.broadcasted_iota(jnp.int32, (8 * tiles, B), 1)
    t_at, r_at = at // 8, at % 8
    top, bottom, middle = [], [], []
    for pair in range(4):
        parts = [0.0, 0.0, 0.0]
        for core in range(2):
            group = share_ref[core, pair, 33 : 33 + tiles].reshape(8 * tiles, B)
            c = cell - core * 2 * tiles
            lev_at = c // tiles
            hit = (c >= 0) & (c < 2 * tiles) & (c % tiles == t_at)
            for half in range(2):
                sel = jnp.where(hit & (r_at == 2 * lev_at + half), 1.0, 0.0).astype(BF16)
                parts[half] = parts[half] + pick_t(group.astype(BF16), sel)
            sel = jnp.where(hit & (r_at == 4 + lev_at), 1.0, 0.0)
            parts[2] = parts[2] + mm(group, sel, TN)[0:1]
        top.append(parts[0])
        bottom.append(parts[1])
        middle.append(parts[2])
    cells = jnp.concatenate([jnp.concatenate(top, 1), jnp.concatenate(bottom, 1)], 0)
    cell_mean = jnp.concatenate(middle, 1)
    index = lax.broadcasted_iota(jnp.int32, (1, cols), 1)
    cells, cell_mean = updated(cells, cell_mean, index % tiles, index // tiles)
    cells_ref[...] = cells.astype(BF16)
    cell_mean = in_three(cell_mean)
    for half in range(n // cols):
        lanes = slice(half * cols, (half + 1) * cols)
        tile, col, level, frac = (
            ref[1:2, lanes] for ref in (tile_ref, col_ref, level_ref, frac_ref)
        )
        spots = [(p % 2, p // 2) for p in range(4 * half, 4 * half + 4)]
        slab = jnp.concatenate([share_ref[c, y, 0:32].reshape(members, B) for c, y in spots], 1)
        mean = jnp.concatenate([share_ref[c, y, 32][0:1] for c, y in spots], 1)
        slab, mean = updated(slab, mean, tile, level)
        wraps, next_tile, _ = after(tile, col, cols, tiles)
        hot = one_hot(cols, jnp.where(wraps, level * tiles + next_tile, -1)).astype(BF16)
        yt_ref[:, lanes] = slab + frac * mm16(cells_ref[...], hot)
        ym_ref[0:1, lanes] = mean + frac * jnp.sum(mm16(cell_mean, hot)[0:8], axis=0, keepdims=True)


def whole_kernel(*refs):
    args, (x_ref, xm_ref), refs = refs[:10], refs[10:12], refs[12:]
    held, refs = refs[:8], refs[8:]
    share0, panel0, share1, panel1, refs = refs[0], refs[1], refs[2], refs[3], refs[4:]
    bufs0, bufs2, bufs1, refs = refs[:7], refs[7:14], refs[14:21], refs[21:]
    (load, send0, recv0, send2, recv2, send1, recv1), refs = refs[:7], refs[7:]
    (yt_ref, ym_ref, cells_ref), scratch = refs[:3], refs[3:]

    barrier = pltpu.get_barrier_semaphore()
    place = Place()
    for peer in place.peers:
        pl.semaphore_signal(barrier, inc=1, device_id=peer, device_id_type=MESH)
    copies = [
        pltpu.make_async_copy(src, dst, load.at[k])
        for k, (src, dst) in enumerate(zip(args, (x_ref, xm_ref) + tuple(held)))
    ]
    for copy in copies:
        copy.start()
    for copy in copies:
        copy.wait()
    val_ref, var_ref, frac_ref, tile_ref, col_ref, level_ref, lh_ref, lv_ref = held
    sites = (tile_ref, col_ref, level_ref, frac_ref)
    levels, members, cols = x_ref.shape

    def put_first(i, values, mean):
        for half in range(2):
            rows = values[half * B : (half + 1) * B]
            share0[i // 4, half, i % 4, 0:16] = rows.reshape(16, 8, B)
            share0[i // 4, half, i % 4, 16] = mean

    def put_second(i, values, mean):
        share1[i % 2, i // 2, 0:32] = values.reshape(32, 8, B)
        share1[i % 2, i // 2, 32] = mean

    gather_sites(0, True, (0, 1), x_ref, xm_ref, sites, put_first)
    pl.semaphore_wait(barrier, len(place.peers))
    early = half_sum_phases(place, share0.at[0], panel0.at[0], bufs0, send0, recv0)
    later = half_sum_phases(place, share0.at[1], panel0.at[1], bufs2, send2, recv2)
    second_sum = sum_phases(place, share1, panel1, bufs1, send1, recv1, True)
    early[0]()
    gather_sites(0, True, (2, 3), x_ref, xm_ref, sites, put_first)
    later[0]()
    gather_sites(1, False, range(4), x_ref, xm_ref, sites, put_second)
    r16 = lax.broadcasted_iota(jnp.int32, (B, B), 0)
    own = jnp.zeros((8, B), F32)
    row = lax.broadcasted_iota(jnp.int32, (8, B), 0)
    for lev in range(levels):
        for half in range(2):
            block = x_ref[lev, half * B : (half + 1) * B, 0:B].astype(F32).T
            own = jnp.where(row == 2 * lev + half, block[0:1], own)
        own = jnp.where(row == 4 + lev, xm_ref[lev : lev + 1, 0:1], own)
    panel1[place.core, place.y, place.cell_home] = own
    early[1]()
    for k in range(2, 7):
        early[k]()
        later[k - 1]()
    early[7]()
    second_sum[0]()

    def damping(batch):
        near = rows8(lh_ref.at[batch], pl.ds(place.home, 1))
        first = lax.axis_index("lev") * levels
        return [near * rows8(lv_ref.at[batch], pl.ds(first + lev, 1)) for lev in range(levels)]

    def between(w_lines):
        second_sum[8]()
        update_sites(panel1, lh_ref, lv_ref, sites, scratch, w_lines, yt_ref, ym_ref, cells_ref)

    def both(one, two):
        def run():
            one()
            two()
        return run

    hooks = second_sum[1:7] + [lambda: None, second_sum[7]]
    hooks[0] = both(later[6], hooks[0])
    hooks[1] = both(later[7], hooks[1])
    analyse(
        lambda i: jnp.concatenate(
            [panel0[i // 4, half, i % 4, 0:16].reshape(B, B) for half in range(2)], axis=0
        ),
        lambda i: panel0[i // 4, 0, i % 4, 16][0:1],
        rows8(val_ref, slice(0, 1)), rows8(var_ref, slice(0, 1)), damping(0), x_ref, xm_ref,
        hooks, between, scratch, 4,
    )
    analyse(
        lambda i: yt_ref[:, i * B : (i + 1) * B],
        lambda i: ym_ref[0:1, i * B : (i + 1) * B],
        rows8(val_ref, slice(1, 2)), rows8(var_ref, slice(1, 2)), damping(1), x_ref, xm_ref,
        [], lambda w_lines: None, scratch, 0,
    )


def analysis_scratch(n, e, cols):
    nb = n // B

    def buf(*shape):
        return pltpu.VMEM(shape, F32)

    return [
        buf(n, e), pltpu.VMEM((n, e), BF16), buf(e, e), buf(nb + 1, e, e), buf(B, B), buf(B, B),
        buf(B, B), buf(B, e), buf(B, e), buf(8, e), buf(n + B, e), buf(nb, B), buf(nb, B),
        buf(nb, B, B), pltpu.VMEM((e, n), BF16), pltpu.VMEM((n, cols), BF16),
    ]


def shards(*args):
    perturb, mean_state, obs_value = args[:3]
    levels, members, cols = perturb.shape
    n = obs_value.shape[1]
    vm = pl.BlockSpec(memory_space=pltpu.VMEM)
    share = pltpu.VMEM((2, 4, members // 8 + 1, 8, B), F32)
    halves = pltpu.VMEM((2, 2, 4, members // 16 + 1, 8, B), F32)
    dma = pltpu.SemaphoreType.DMA
    return pl.pallas_call(
        whole_kernel,
        out_shape=(
            jax.ShapeDtypeStruct(perturb.shape, BF16),
            jax.ShapeDtypeStruct(mean_state.shape, F32),
        ),
        in_specs=[pl.BlockSpec(memory_space=pltpu.HBM)] * len(args),
        out_specs=(vm, vm),
        scratch_shapes=[pltpu.VMEM(a.shape, a.dtype) for a in args[2:]]
        + [halves, halves, share, pltpu.VMEM((2, 4, members // 8 + 33, 8, B), F32)]
        + half_sum_buffers()
        + half_sum_buffers()
        + sum_buffers()
        + [dma((len(args),))] + [dma((COPIES,))] * 6
        + [pltpu.VMEM((members, n), F32), pltpu.VMEM((8, n), F32), pltpu.VMEM((members, cols), BF16)]
        + analysis_scratch(n, members, cols),
        compiler_params=pltpu.CompilerParams(
            collective_id=0, has_side_effects=True, vmem_limit_bytes=60 * 2**20
        ),
        name="analysis",
    )(*args)


def solution(mesh):
    return jax.shard_map(
        shards,
        mesh=mesh,
        in_specs=(P("lev", None, "horiz"), P("lev", "horiz")) + (P(),) * 8,
        out_specs=(P("lev", None, "horiz"), P("lev", "horiz")),
        check_vma=False,
    )
```

```python
import functools
import jax
import jax.numpy as jnp
from jax import lax
from jax.experimental import pallas as pl
from jax.experimental.pallas import tpu as pltpu
from jax.sharding import PartitionSpec as P

F32 = jnp.float32
BF16 = jnp.bfloat16
HIGHEST = lax.Precision.HIGHEST
MESH = pl.DeviceIdType.MESH
B = 128
SUB = 16
Q = 64
NT = ((1,), (1,))
TN = ((0,), (0,))
NN = ((1,), (0,))


def mm(a, b, dims=NN):
    return lax.dot_general(a, b, (dims, ((), ())), precision=HIGHEST, preferred_element_type=F32)


def mm16(a, b):
    return jnp.dot(a, b, preferred_element_type=F32)


def columns_of(rows):
    return jnp.concatenate([rows] * 16, axis=0).T


def rows_at(i):
    return pl.ds(pl.multiple_of(i * B, B), B)


def in_three(rows):
    hi = rows.astype(BF16).astype(F32)
    mid = (rows - hi).astype(BF16).astype(F32)
    low = rows - hi - mid
    at = lax.broadcasted_iota(jnp.int32, (16, rows.shape[1]), 0)
    return jnp.where(at == 0, hi, jnp.where(at == 1, mid, jnp.where(at == 2, low, 0.0))).astype(BF16)


def one_hot(rows, index):
    at = lax.broadcasted_iota(jnp.int32, (rows, index.shape[1]), 0)
    return jnp.where(at == index, 1.0, 0.0)


def after(tile, col, cols, tiles):
    wraps = col == cols - 1
    next_tile = jnp.where(wraps, jnp.where(tile == tiles - 1, 0, tile + 1), tile)
    return wraps, next_tile, jnp.where(wraps, 0, col + 1)


def gather_sites(batch, across, quarters, x_ref, xm_ref, sites, put):
    tile_ref, col_ref, level_ref, frac_ref = sites
    levels, members, cols = x_ref.shape
    tiles = lax.axis_size("horiz")
    my_tile = lax.axis_index("horiz")
    first = lax.axis_index("lev") * levels
    row = lax.broadcasted_iota(jnp.int32, (8, B), 0)
    width = 2 * B
    means = [in_three(xm_ref[lev : lev + 1, :]) for lev in range(levels)]
    for jb in quarters:
        lanes = slice(jb * width, (jb + 1) * width)
        tile, col, level, frac = (
            ref[batch : batch + 1, lanes] for ref in (tile_ref, col_ref, level_ref, frac_ref)
        )
        wraps, next_tile, next_col = after(tile, col, cols, tiles)
        if not across:
            next_col = jnp.where(wraps, -1, next_col)
        vals = []
        for t, c in ((tile, col), (next_tile, next_col)):
            v = jnp.zeros((members, width), F32)
            m = jnp.zeros((16, width), F32)
            for lev in range(levels):
                pos = jnp.where((t == my_tile) & (level == first + lev), c, -1)
                hot = one_hot(cols, pos).astype(BF16)
                v = v + mm16(x_ref[lev], hot)
                m = m + mm16(means[lev], hot)
            vals.append((v, jnp.sum(m[0:8], axis=0, keepdims=True)))
        site = (1.0 - frac) * vals[0][0] + frac * vals[1][0]
        mean = (1.0 - frac) * vals[0][1] + frac * vals[1][1]
        for core in range(2):
            half = slice(core * B, (core + 1) * B)
            put(2 * jb + core, site[:, half], jnp.where(row == 0, mean[:, half], 0.0))


class Place:
    def __init__(self):
        horiz = lax.axis_index("horiz")
        lev = lax.axis_index("lev")
        self.x, self.z = horiz // 8, horiz % 8
        self.y, self.core = lev // 2, lev % 2
        self.other = 1 - self.core
        self.xs = [self.x] + [(self.x + k) % 4 for k in range(1, 4)]
        self.ys = [self.y] + [(self.y + k) % 4 for k in range(1, 4)]
        self.ys_back = [self.y] + [(self.y - k + 4) % 4 for k in range(1, 4)]
        self.zs = [self.z] + [(self.z + k) % 8 for k in range(1, 8)]
        self.to_core = (horiz, self.y * 2 + self.other)
        self.to_y = [None] + [(horiz, self.ys[k] * 2 + self.core) for k in range(1, 4)]
        self.to_x = [None] + [(self.xs[k] * 8 + self.z, lev) for k in range(1, 4)]
        self.to_z = [None] + [(self.x * 8 + self.zs[k], lev) for k in range(1, 8)]
        self.peers = [self.to_core] + self.to_y[1:] + self.to_x[1:] + self.to_z[1:]
        self.home = 8 * self.x + self.z
        self.x8 = 8 * self.x
        self.xs8 = [8 * v for v in self.xs]
        self.cell_home = 33 + self.home
        self.cell_x8 = 33 + self.x8
        self.zs2 = [2 * v for v in self.zs]


def sum_phases(place, c_ref, o_ref, bufs, send, recv, cells):
    r0, a0, r1, a1, r2, a2, r3 = bufs
    core, other, x, y, z = place.core, place.other, place.x, place.y, place.z
    sem = iter(range(COPIES))

    def copy(src, dst, peer):
        k = next(sem)
        return lambda: pltpu.make_async_remote_copy(
            src_ref=src, dst_ref=dst, send_sem=send.at[k], recv_sem=recv.at[k],
            device_id=peer, device_id_type=MESH,
        )

    order = (1, 2, 3, 0)
    to_core = [
        copy(c_ref.at[other, place.ys[k]], r0.at[place.ys[k]], place.to_core) for k in order
    ]
    to_y = [copy(a0.at[place.ys[k]], r1.at[k - 1], place.to_y[k]) for k in range(1, 4)]
    to_x, to_z, back_z, back_x = [], [], [], []
    for k in range(1, 4):
        to_x.append(copy(a1.at[pl.ds(place.xs8[k], 8)], r2.at[k - 1, pl.ds(0, 8)], place.to_x[k]))
        to_x.append(copy(a1.at[pl.ds(32, 1)], r2.at[k - 1, pl.ds(8, 1)], place.to_x[k]))
    for k in range(1, 8):
        to_z.append(copy(a2.at[pl.ds(place.zs[k], 1)], r3.at[k - 1, pl.ds(0, 1)], place.to_z[k]))
        to_z.append(copy(a2.at[pl.ds(8, 1)], r3.at[k - 1, pl.ds(1, 1)], place.to_z[k]))
    starts = (place.home, place.cell_home) if cells else (place.home,)
    for k in range(1, 8):
        for s in starts:
            spot = o_ref.at[core, y, pl.ds(s, 1)]
            back_z.append(copy(spot, spot, place.to_z[k]))
    starts = (place.x8, place.cell_x8) if cells else (place.x8,)
    for k in range(1, 4):
        for s in starts:
            spot = o_ref.at[core, y, pl.ds(s, 8)]
            back_x.append(copy(spot, spot, place.to_x[k]))
    spot = o_ref.at[core, y]
    back_y = [copy(spot, spot, place.to_y[k]) for k in range(1, 4)]
    back_core = []
    for k in range(4):
        spot = o_ref.at[core, place.ys_back[k]]
        back_core.append(copy(spot, spot, place.to_core))

    def start(copies):
        for c in copies:
            c().start()

    def arrive(copies):
        for c in copies:
            c().wait_recv()

    def begin():
        start(to_core)

    def add_core():
        for k, c in zip(order, to_core):
            c().wait_recv()
            yk = place.ys[k]
            a0[yk] = c_ref[core, yk] + r0[yk]
            if k:
                to_y[k - 1]().start()

    def add_y():
        arrive(to_y)
        a1[...] = (a0[y] + r1[0]) + (r1[1] + r1[2])
        start(to_x)

    def add_x():
        arrive(to_x)
        a2[0:8] = (a1[pl.ds(place.x8, 8)] + r2[0, 0:8]) + (r2[1, 0:8] + r2[2, 0:8])
        a2[8:9] = (a1[32:33] + r2[0, 8:9]) + (r2[1, 8:9] + r2[2, 8:9])
        start(to_z)

    def add_z():
        arrive(to_z)
        mine = a2[z]
        mean = a2[8]
        for k in range(7):
            mine = mine + r3[k, 0]
            mean = mean + r3[k, 1]
        o_ref[core, y, place.home] = mine
        o_ref[core, y, 32] = mean
        start(back_z)

    def return_x():
        arrive(back_z)
        start(back_x)

    def return_y():
        arrive(back_x)
        start(back_y)
        start(back_core[:1])

    def return_core():
        for k in range(3):
            back_y[k]().wait_recv()
            back_core[k + 1]().start()

    def end():
        arrive(back_core)
        for group in (to_core, to_y, to_x, to_z, back_z, back_x, back_y, back_core):
            for c in group:
                c().wait_send()

    return [begin, add_core, add_y, add_x, add_z, return_x, return_y, return_core, end]


def half_sum_phases(place, c_ref, o_ref, bufs, send, recv):
    r0, a0, r1, a1, r2, a2, r3 = bufs
    core, other, y = place.core, place.other, place.y
    sem = iter(range(COPIES))

    def copy(src, dst, peer):
        k = next(sem)
        return lambda: pltpu.make_async_remote_copy(
            src_ref=src, dst_ref=dst, send_sem=send.at[k], recv_sem=recv.at[k],
            device_id=peer, device_id_type=MESH,
        )

    order = (1, 2, 3, 0)
    to_core = [
        copy(c_ref.at[other, place.ys[k]], r0.at[place.ys[k]], place.to_core) for k in order
    ]
    to_y = [copy(a0.at[place.ys[k]], r1.at[k - 1], place.to_y[k]) for k in range(1, 4)]
    to_z, back_z = [], []
    for k in range(1, 8):
        to_z.append(copy(a1.at[pl.ds(place.zs2[k], 2)], r2.at[k - 1, pl.ds(0, 2)], place.to_z[k]))
        to_z.append(copy(a1.at[pl.ds(16, 1)], r2.at[k - 1, pl.ds(2, 1)], place.to_z[k]))
    to_x = [copy(a2, r3.at[k - 1], place.to_x[k]) for k in range(1, 4)]
    for k in range(1, 8):
        spot = o_ref.at[core, y, pl.ds(place.zs2[0], 2)]
        back_z.append(copy(spot, spot, place.to_z[k]))
    spot = o_ref.at[core, y]
    back_y = [copy(spot, spot, place.to_y[k]) for k in range(1, 4)]
    back_core = []
    for k in range(4):
        spot = o_ref.at[core, place.ys_back[k]]
        back_core.append(copy(spot, spot, place.to_core))

    def start(copies):
        for c in copies:
            c().start()

    def arrive(copies):
        for c in copies:
            c().wait_recv()

    def begin():
        start(to_core)

    def add_core():
        for k, c in zip(order, to_core):
            c().wait_recv()
            yk = place.ys[k]
            a0[yk] = c_ref[core, yk] + r0[yk]
            if k:
                to_y[k - 1]().start()

    def add_y():
        arrive(to_y)
        a1[...] = (a0[y] + r1[0]) + (r1[1] + r1[2])
        start(to_z)

    def add_z():
        arrive(to_z)
        mine = a1[pl.ds(place.zs2[0], 2)]
        mean = a1[16:17]
        for k in range(7):
            mine = mine + r2[k, 0:2]
            mean = mean + r2[k, 2:3]
        a2[0:2] = mine
        a2[2:3] = mean
        start(to_x)

    def add_x():
        arrive(to_x)
        total = (a2[...] + r3[0]) + (r3[1] + r3[2])
        o_ref[core, y, pl.ds(place.zs2[0], 2)] = total[0:2]
        o_ref[core, y, 16] = total[2]
        start(back_z)

    def return_y():
        arrive(back_z)
        start(back_y)
        start(back_core[:1])

    def return_core():
        for k in range(3):
            back_y[k]().wait_recv()
            back_core[k + 1]().start()

    def end():
        arrive(back_core)
        for group in (to_core, to_y, to_z, to_x, back_z, back_y, back_core):
            for c in group:
                c().wait_send()

    return [begin, add_core, add_y, add_z, add_x, return_y, return_core, end]


COPIES = 4 + 3 + 6 + 14 + 14 + 6 + 3 + 4


def sum_buffers():
    def buf(*shape):
        return pltpu.VMEM(shape + (8, B), F32)

    return [buf(4, 33), buf(4, 33), buf(3, 33), buf(33), buf(3, 9), buf(9), buf(7, 2)]


def half_sum_buffers():
    def buf(*shape):
        return pltpu.VMEM(shape + (8, B), F32)

    return [buf(4, 17), buf(4, 17), buf(3, 17), buf(17), buf(7, 3), buf(3), buf(3, 3)]


def factor_block(s, dcol):
    nt = Q // 8
    row = lax.broadcasted_iota(jnp.int32, (8, B), 0)
    lane = lax.broadcasted_iota(jnp.int32, (8, B), 1)
    eye = jnp.where(
        lax.broadcasted_iota(jnp.int32, (B, B), 0) == lax.broadcasted_iota(jnp.int32, (B, B), 1),
        1.0,
        0.0,
    )
    both, shifted = s, eye
    out_a, out_z = [], []
    for o in range(0, B, Q):
        w_t = [both[8 * t : 8 * t + 8] for t in range(nt)]
        z_t = [shifted[8 * t : 8 * t + 8] for t in range(nt)]
        for sub in range(0, Q, SUB):
            begin, end = o + sub, o + sub + SUB
            own = (lane >= begin) & (lane < end)
            cols = {}
            for c in range(sub, sub + SUB):
                cols[c] = [
                    None if t < c // 8 else jnp.broadcast_to(w_t[t][:, o + c : o + c + 1], (8, B))
                    for t in range(nt)
                ]
            for t in range(sub // 8, nt):
                unit = lane == row + (o + 8 * t)
                if t < (sub + SUB) // 8:
                    w_t[t] = jnp.where(own, jnp.where(unit, 1.0, 0.0), w_t[t])
                else:
                    w_t[t] = jnp.where(own, 0.0, w_t[t])
            for r in range(sub, sub + SUB):
                tr, rr = r // 8, r % 8
                p = cols[r][tr][rr : rr + 1]
                rs = lax.rsqrt(p)
                l = [None if t < tr else cols[r][t] * rs for t in range(nt)]
                for c in range(r + 1, sub + SUB):
                    f = l[c // 8][c % 8 : c % 8 + 1]
                    for t in range(c // 8, nt):
                        cols[c][t] = cols[c][t] - l[t] * f
                scale = 1.0 / (p * rs + dcol[o + r : o + r + 1])
                for rows, v in ((w_t, w_t[tr][rr : rr + 1] * rs), (z_t, z_t[tr][rr : rr + 1] * scale)):
                    for t in range(tr, nt):
                        lt = l[t] if t > tr else jnp.where(row > rr, l[t], 0.0)
                        new = rows[t] - lt * v
                        if t == tr:
                            new = jnp.where(row == rr, jnp.broadcast_to(v, (8, B)), new)
                        rows[t] = new
            if sub + SUB < Q:
                ahead = (lane >= end) & (lane < o + Q)
                for t in range(sub // 8, (sub + SUB) // 8):
                    w_t[t] = jnp.where(ahead, 0.0, w_t[t])
        u_b, z_b = jnp.concatenate(w_t, 0), jnp.concatenate(z_t, 0)
        out_a.append(jnp.where(lax.broadcasted_iota(jnp.int32, (Q, B), 1) < o + Q, u_b, 0.0))
        out_z.append(z_b)
        if o + Q < B:
            step = mm(u_b, jnp.concatenate([u_b, z_b], 1), TN)[o + Q :]
            at = lax.broadcasted_iota(jnp.int32, (B - o - Q, B), 1)
            both = jnp.where((at >= o) & (at < o + Q), 0.0, both[Q:]) - step[:, :B]
            shifted = shifted[Q:] - step[:, B:]
    return jnp.concatenate(out_a, 0), jnp.concatenate(out_z, 0)


def rows8(ref, row):
    line = ref[row, :]
    return jnp.concatenate([line[:, k : k + B] for k in range(0, line.shape[1], B)], axis=0)


def analyse(site_of, mean_of, values, variances, damping, x_ref, xm_ref, hooks, between, scratch,
            late):
    (a_ref, yb_ref, p_ref, qs_ref, s_ref, linv_ref, minv_ref, t1_ref, aq_ref, lz_ref,
     d_ref, var_ref, vcol_ref, gt_ref, k_ref) = scratch
    levels, members, cols = x_ref.shape
    n = a_ref.shape[0]
    nb = n // B
    c = 1.0 / (members - 1.0) ** 0.5

    def square(k):
        return lax.broadcasted_iota(jnp.int32, (k, k), 0) == lax.broadcasted_iota(
            jnp.int32, (k, k), 1
        )

    eye_m = jnp.where(square(members), 1.0, 0.0)
    diag = square(B)
    def fill(blocks):
        for i in blocks:
            y_i = site_of(i).T
            a_ref[i * B : (i + 1) * B] = y_i * c
            yb_ref[i * B : (i + 1) * B] = y_i.astype(BF16)
            d_ref[i : i + 1] = values[i : i + 1] - mean_of(i)

    fill(range(nb - late))
    var_ref[...] = variances
    var_cols = columns_of(variances)
    for i in range(nb):
        vcol_ref[i] = jnp.broadcast_to(var_cols[:, i : i + 1], (B, B))
    p_ref[...] = eye_m
    qs_ref[0] = eye_m * (1.0 / c)
    a_0 = a_ref[0:B]
    s_ref[...] = mm(a_0, a_0, NT) + jnp.where(diag, var_ref[0:1], 0.0)
    for ref in (linv_ref, minv_ref, t1_ref, aq_ref):
        ref[...] = jnp.zeros_like(ref)

    def finish_previous(i):
        linv, minv, t1 = linv_ref[...], minv_ref[...], t1_ref[...]
        ip = jnp.maximum(i - 1, 0)
        v = mm(linv, t1)
        z = mm(minv, aq_ref[...])
        lz_ref[rows_at(i)] = mm(linv, z, TN)
        p = p_ref[...] - mm(v, v, TN)
        q = qs_ref[ip] - mm(v, z, TN)
        return p, q

    def step(i, carry):
        p, q = finish_previous(i)
        i_next = jnp.minimum(i + 1, nb - 1)
        a_i = a_ref[rows_at(i)]
        a_n = a_ref[rows_at(i_next)]
        t1 = mm(a_i, p)
        t1_n = mm(a_n, p)
        s_nn = mm(t1_n, a_n, NT) + jnp.where(diag, var_ref[pl.ds(i_next, 1)], 0.0)
        s_in = mm(a_i, t1_n, NT)
        aq = mm(a_i, q)
        linv, minv = factor_block(s_ref[...], jnp.sqrt(vcol_ref[i]))
        l_in = mm(linv, s_in)
        s_ref[...] = s_nn - mm(l_in, l_in, TN)
        linv_ref[...] = linv
        minv_ref[...] = minv
        t1_ref[...] = t1
        aq_ref[...] = aq
        p_ref[...] = p
        qs_ref[i] = q
        for k, hook in enumerate(hooks):
            pl.when(i == k)(hook)
        if late:
            pl.when(i == nb - late - 2)(lambda: fill(range(nb - late, nb)))
        return carry

    lax.fori_loop(0, nb, step, 0)
    p, q = finish_previous(nb)

    d_cols = columns_of(d_ref[...])
    inv_var = [1.0 / vcol_ref[i] for i in range(nb)]

    def over_obs(lines):
        total = 0.0
        for i in range(nb):
            part = a_ref[i * B : (i + 1) * B] * lines[i]
            total = total + jnp.sum(part.reshape(B // 8, 8, members), axis=0)
        return jnp.sum(total, axis=0, keepdims=True)

    def times_a(v):
        return [
            jnp.sum(a_ref[i * B : (i + 1) * B] * v, axis=1, keepdims=True) for i in range(nb)
        ]

    def solve_for(rest):
        v = over_obs([r * inv[:, 0:1] for r, inv in zip(rest, inv_var)])
        back = times_a(mm(jnp.broadcast_to(v, (8, members)), p)[0:1])
        return [(r - t) * inv[:, 0:1] for r, t, inv in zip(rest, back, inv_var)]

    d_lines = [d_cols[:, i : i + 1] for i in range(nb)]
    w_lines = solve_for(d_lines)
    for _ in range(1):
        back = times_a(over_obs(w_lines))
        rest = [
            d - vcol_ref[i][:, 0:1] * w - t
            for i, (d, w, t) in enumerate(zip(d_lines, w_lines, back))
        ]
        w_lines = [w + more for w, more in zip(w_lines, solve_for(rest))]

    for i in range(nb):
        g = lz_ref[(i + 1) * B : (i + 2) * B]
        if i < nb - 1:
            inv = 1.0 / vcol_ref[i]
            g = g - mm(a_ref[i * B : (i + 1) * B], qs_ref[i + 1] - q) * jnp.concatenate([inv, inv], 1)
        gt_ref[:, i * B : (i + 1) * B] = g.T.astype(BF16)

    between(w_lines)
    for lev in range(levels):
        damp_cols = columns_of(damping[lev] * (1.0 / (members - 1.0)))
        slab = x_ref[lev]
        inc, mean = increments(
            lambda i: mm16(yb_ref[i * B : (i + 1) * B], slab) * damp_cols[:, i : i + 1],
            w_lines, gt_ref, k_ref,
        )
        xm_ref[lev : lev + 1] = xm_ref[lev : lev + 1] + mean
        x_ref[lev] = (slab.astype(F32) - inc).astype(BF16)


def increments(gain_of, w_lines, gt_ref, k_ref):
    mean = 0.0
    for i, w in enumerate(w_lines):
        f = gain_of(i)
        k_ref[i * B : (i + 1) * B] = f.astype(BF16)
        mean = mean + jnp.sum((f * w).reshape(B // 8, 8, f.shape[1]), axis=0)
    inc = [mm16(gt_ref[...], k_ref[:, c : c + 256]) for c in range(0, k_ref.shape[1], 256)]
    return jnp.concatenate(inc, axis=1), jnp.sum(mean, axis=0, keepdims=True)


def stack_three(rows):
    hi = rows.astype(BF16)
    mid = (rows - hi.astype(F32)).astype(BF16)
    low = (rows - hi.astype(F32) - mid.astype(F32)).astype(BF16)
    return jnp.concatenate([hi, mid, low], axis=0)


def pick_t(table, hot):
    return lax.dot_general(table, hot, (TN, ((), ())), preferred_element_type=F32)


def update_sites(share_ref, lh_ref, lv_ref, sites, scratch, w_lines, yt_ref, ym_ref, cells_ref):
    tile_ref, col_ref, level_ref, frac_ref = sites
    yb_ref, gt_ref, k_ref = scratch[1], scratch[13], scratch[14]
    n, members = yb_ref.shape
    cols = k_ref.shape[1]
    tiles, levels = lh_ref.shape[1], lv_ref.shape[1]
    lh = stack_three(lh_ref[0] * (1.0 / (members - 1.0)))
    lv = stack_three(lv_ref[0])

    def updated(slab, mean, tile, level):
        hi = slab.astype(BF16)
        low = (slab - hi.astype(F32)).astype(BF16)
        hot_t = one_hot(tiles, tile).astype(BF16)
        hot_l = one_hot(levels, level).astype(BF16)
        hot_t = jnp.concatenate([hot_t] * 3, axis=0)
        hot_l = jnp.concatenate([hot_l] * 3, axis=0)

        def gain_of(i):
            y_i = yb_ref[i * B : (i + 1) * B]
            damp = pick_t(lh[:, i * B : (i + 1) * B], hot_t) * pick_t(lv[:, i * B : (i + 1) * B], hot_l)
            return (mm16(y_i, hi) + mm16(y_i, low)) * damp

        inc, gained = increments(gain_of, w_lines, gt_ref, k_ref)
        return slab - inc, mean + gained

    at = lax.broadcasted_iota(jnp.int32, (8 * tiles, B), 0)
    cell = lax.broadcasted_iota(jnp.int32, (8 * tiles, B), 1)
    t_at, r_at = at // 8, at % 8
    top, bottom, middle = [], [], []
    for pair in range(4):
        parts = [0.0, 0.0, 0.0]
        for core in range(2):
            group = share_ref[core, pair, 33 : 33 + tiles].reshape(8 * tiles, B)
            c = cell - core * 2 * tiles
            lev_at = c // tiles
            hit = (c >= 0) & (c < 2 * tiles) & (c % tiles == t_at)
            for half in range(2):
                sel = jnp.where(hit & (r_at == 2 * lev_at + half), 1.0, 0.0).astype(BF16)
                parts[half] = parts[half] + pick_t(group.astype(BF16), sel)
            sel = jnp.where(hit & (r_at == 4 + lev_at), 1.0, 0.0)
            parts[2] = parts[2] + mm(group, sel, TN)[0:1]
        top.append(parts[0])
        bottom.append(parts[1])
        middle.append(parts[2])
    cells = jnp.concatenate([jnp.concatenate(top, 1), jnp.concatenate(bottom, 1)], 0)
    cell_mean = jnp.concatenate(middle, 1)
    index = lax.broadcasted_iota(jnp.int32, (1, cols), 1)
    cells, cell_mean = updated(cells, cell_mean, index % tiles, index // tiles)
    cells_ref[...] = cells.astype(BF16)
    cell_mean = in_three(cell_mean)
    for half in range(n // cols):
        lanes = slice(half * cols, (half + 1) * cols)
        tile, col, level, frac = (
            ref[1:2, lanes] for ref in (tile_ref, col_ref, level_ref, frac_ref)
        )
        spots = [(p % 2, p // 2) for p in range(4 * half, 4 * half + 4)]
        slab = jnp.concatenate([share_ref[c, y, 0:32].reshape(members, B) for c, y in spots], 1)
        mean = jnp.concatenate([share_ref[c, y, 32][0:1] for c, y in spots], 1)
        slab, mean = updated(slab, mean, tile, level)
        wraps, next_tile, _ = after(tile, col, cols, tiles)
        hot = one_hot(cols, jnp.where(wraps, level * tiles + next_tile, -1)).astype(BF16)
        yt_ref[:, lanes] = slab + frac * mm16(cells_ref[...], hot)
        ym_ref[0:1, lanes] = mean + frac * jnp.sum(mm16(cell_mean, hot)[0:8], axis=0, keepdims=True)


def whole_kernel(*refs):
    args, (x_ref, xm_ref), refs = refs[:10], refs[10:12], refs[12:]
    held, refs = refs[:8], refs[8:]
    share0, panel0, share1, panel1, refs = refs[0], refs[1], refs[2], refs[3], refs[4:]
    bufs0, bufs2, bufs1, refs = refs[:7], refs[7:14], refs[14:21], refs[21:]
    (load, send0, recv0, send2, recv2, send1, recv1), refs = refs[:7], refs[7:]
    (yt_ref, ym_ref, cells_ref), scratch = refs[:3], refs[3:]

    barrier = pltpu.get_barrier_semaphore()
    place = Place()
    for peer in place.peers:
        pl.semaphore_signal(barrier, inc=1, device_id=peer, device_id_type=MESH)
    copies = [
        pltpu.make_async_copy(src, dst, load.at[k])
        for k, (src, dst) in enumerate(zip(args, (x_ref, xm_ref) + tuple(held)))
    ]
    for copy in copies:
        copy.start()
    for copy in copies:
        copy.wait()
    val_ref, var_ref, frac_ref, tile_ref, col_ref, level_ref, lh_ref, lv_ref = held
    sites = (tile_ref, col_ref, level_ref, frac_ref)
    levels, members, cols = x_ref.shape

    def put_first(i, values, mean):
        for half in range(2):
            rows = values[half * B : (half + 1) * B]
            share0[i // 4, half, i % 4, 0:16] = rows.reshape(16, 8, B)
            share0[i // 4, half, i % 4, 16] = mean

    def put_second(i, values, mean):
        share1[i % 2, i // 2, 0:32] = values.reshape(32, 8, B)
        share1[i % 2, i // 2, 32] = mean

    gather_sites(0, True, (0, 1), x_ref, xm_ref, sites, put_first)
    pl.semaphore_wait(barrier, len(place.peers))
    early = half_sum_phases(place, share0.at[0], panel0.at[0], bufs0, send0, recv0)
    later = half_sum_phases(place, share0.at[1], panel0.at[1], bufs2, send2, recv2)
    second_sum = sum_phases(place, share1, panel1, bufs1, send1, recv1, True)
    early[0]()
    gather_sites(0, True, (2, 3), x_ref, xm_ref, sites, put_first)
    later[0]()
    gather_sites(1, False, range(4), x_ref, xm_ref, sites, put_second)
    r16 = lax.broadcasted_iota(jnp.int32, (B, B), 0)
    own = jnp.zeros((8, B), F32)
    row = lax.broadcasted_iota(jnp.int32, (8, B), 0)
    for lev in range(levels):
        for half in range(2):
            block = x_ref[lev, half * B : (half + 1) * B, 0:B].astype(F32).T
            own = jnp.where(row == 2 * lev + half, block[0:1], own)
        own = jnp.where(row == 4 + lev, xm_ref[lev : lev + 1, 0:1], own)
    panel1[place.core, place.y, place.cell_home] = own
    early[1]()
    for k in range(2, 7):
        early[k]()
        later[k - 1]()
    early[7]()
    second_sum[0]()

    def damping(batch):
        near = rows8(lh_ref.at[batch], pl.ds(place.home, 1))
        first = lax.axis_index("lev") * levels
        return [near * rows8(lv_ref.at[batch], pl.ds(first + lev, 1)) for lev in range(levels)]

    def between(w_lines):
        second_sum[8]()
        update_sites(panel1, lh_ref, lv_ref, sites, scratch, w_lines, yt_ref, ym_ref, cells_ref)

    def both(one, two):
        def run():
            one()
            two()
        return run

    hooks = second_sum[1:7] + [lambda: None, second_sum[7]]
    hooks[0] = both(later[6], hooks[0])
    hooks[1] = both(later[7], hooks[1])
    analyse(
        lambda i: jnp.concatenate(
            [panel0[i // 4, half, i % 4, 0:16].reshape(B, B) for half in range(2)], axis=0
        ),
        lambda i: panel0[i // 4, 0, i % 4, 16][0:1],
        rows8(val_ref, slice(0, 1)), rows8(var_ref, slice(0, 1)), damping(0), x_ref, xm_ref,
        hooks, between, scratch, 4,
    )
    analyse(
        lambda i: yt_ref[:, i * B : (i + 1) * B],
        lambda i: ym_ref[0:1, i * B : (i + 1) * B],
        rows8(val_ref, slice(1, 2)), rows8(var_ref, slice(1, 2)), damping(1), x_ref, xm_ref,
        [], lambda w_lines: None, scratch, 0,
    )


def analysis_scratch(n, e, cols):
    nb = n // B

    def buf(*shape):
        return pltpu.VMEM(shape, F32)

    return [
        buf(n, e), pltpu.VMEM((n, e), BF16), buf(e, e), buf(nb + 1, e, e), buf(B, B), buf(B, B),
        buf(B, B), buf(B, e), buf(B, e), buf(n + B, e), buf(nb, B), buf(nb, B),
        buf(nb, B, B), pltpu.VMEM((e, n), BF16), pltpu.VMEM((n, cols), BF16),
    ]


def shards(*args):
    perturb, mean_state, obs_value = args[:3]
    levels, members, cols = perturb.shape
    n = obs_value.shape[1]
    vm = pl.BlockSpec(memory_space=pltpu.VMEM)
    share = pltpu.VMEM((2, 4, members // 8 + 1, 8, B), F32)
    halves = pltpu.VMEM((2, 2, 4, members // 16 + 1, 8, B), F32)
    dma = pltpu.SemaphoreType.DMA
    return pl.pallas_call(
        whole_kernel,
        out_shape=(
            jax.ShapeDtypeStruct(perturb.shape, BF16),
            jax.ShapeDtypeStruct(mean_state.shape, F32),
        ),
        in_specs=[pl.BlockSpec(memory_space=pltpu.HBM)] * len(args),
        out_specs=(vm, vm),
        scratch_shapes=[pltpu.VMEM(a.shape, a.dtype) for a in args[2:]]
        + [halves, halves, share, pltpu.VMEM((2, 4, members // 8 + 33, 8, B), F32)]
        + half_sum_buffers()
        + half_sum_buffers()
        + sum_buffers()
        + [dma((len(args),))] + [dma((COPIES,))] * 6
        + [pltpu.VMEM((members, n), F32), pltpu.VMEM((8, n), F32), pltpu.VMEM((members, cols), BF16)]
        + analysis_scratch(n, members, cols),
        compiler_params=pltpu.CompilerParams(
            collective_id=0, has_side_effects=True, vmem_limit_bytes=60 * 2**20
        ),
        name="analysis",
    )(*args)


def solution(mesh):
    return jax.shard_map(
        shards,
        mesh=mesh,
        in_specs=(P("lev", None, "horiz"), P("lev", "horiz")) + (P(),) * 8,
        out_specs=(P("lev", None, "horiz"), P("lev", "horiz")),
        check_vma=False,
    )
```

```python
import functools
import jax
import jax.numpy as jnp
from jax import lax
from jax.experimental import pallas as pl
from jax.experimental.pallas import tpu as pltpu
from jax.sharding import PartitionSpec as P

F32 = jnp.float32
BF16 = jnp.bfloat16
HIGHEST = lax.Precision.HIGHEST
MESH = pl.DeviceIdType.MESH
B = 128
SUB = 16
Q = 64
NT = ((1,), (1,))
TN = ((0,), (0,))
NN = ((1,), (0,))


def mm(a, b, dims=NN):
    return lax.dot_general(a, b, (dims, ((), ())), precision=HIGHEST, preferred_element_type=F32)


def mm16(a, b):
    return jnp.dot(a, b, preferred_element_type=F32)


def columns_of(rows):
    return jnp.concatenate([rows] * 16, axis=0).T


def rows_at(i):
    return pl.ds(pl.multiple_of(i * B, B), B)


def in_three(rows):
    hi = rows.astype(BF16).astype(F32)
    mid = (rows - hi).astype(BF16).astype(F32)
    low = rows - hi - mid
    at = lax.broadcasted_iota(jnp.int32, (16, rows.shape[1]), 0)
    return jnp.where(at == 0, hi, jnp.where(at == 1, mid, jnp.where(at == 2, low, 0.0))).astype(BF16)


def one_hot(rows, index):
    at = lax.broadcasted_iota(jnp.int32, (rows, index.shape[1]), 0)
    return jnp.where(at == index, 1.0, 0.0)


def after(tile, col, cols, tiles):
    wraps = col == cols - 1
    next_tile = jnp.where(wraps, jnp.where(tile == tiles - 1, 0, tile + 1), tile)
    return wraps, next_tile, jnp.where(wraps, 0, col + 1)


def gather_sites(batch, across, quarters, x_ref, xm_ref, sites, put):
    tile_ref, col_ref, level_ref, frac_ref = sites
    levels, members, cols = x_ref.shape
    tiles = lax.axis_size("horiz")
    my_tile = lax.axis_index("horiz")
    first = lax.axis_index("lev") * levels
    row = lax.broadcasted_iota(jnp.int32, (8, B), 0)
    width = 2 * B
    means = [in_three(xm_ref[lev : lev + 1, :]) for lev in range(levels)]
    for jb in quarters:
        lanes = slice(jb * width, (jb + 1) * width)
        tile, col, level, frac = (
            ref[batch : batch + 1, lanes] for ref in (tile_ref, col_ref, level_ref, frac_ref)
        )
        wraps, next_tile, next_col = after(tile, col, cols, tiles)
        if not across:
            next_col = jnp.where(wraps, -1, next_col)
        vals = []
        for t, c in ((tile, col), (next_tile, next_col)):
            v = jnp.zeros((members, width), F32)
            m = jnp.zeros((16, width), F32)
            for lev in range(levels):
                pos = jnp.where((t == my_tile) & (level == first + lev), c, -1)
                hot = one_hot(cols, pos).astype(BF16)
                v = v + mm16(x_ref[lev], hot)
                m = m + mm16(means[lev], hot)
            vals.append((v, jnp.sum(m[0:8], axis=0, keepdims=True)))
        site = (1.0 - frac) * vals[0][0] + frac * vals[1][0]
        mean = (1.0 - frac) * vals[0][1] + frac * vals[1][1]
        for core in range(2):
            half = slice(core * B, (core + 1) * B)
            put(2 * jb + core, site[:, half], jnp.where(row == 0, mean[:, half], 0.0))


class Place:
    def __init__(self):
        horiz = lax.axis_index("horiz")
        lev = lax.axis_index("lev")
        self.x, self.z = horiz // 8, horiz % 8
        self.y, self.core = lev // 2, lev % 2
        self.other = 1 - self.core
        self.xs = [self.x] + [(self.x + k) % 4 for k in range(1, 4)]
        self.ys = [self.y] + [(self.y + k) % 4 for k in range(1, 4)]
        self.ys_back = [self.y] + [(self.y - k + 4) % 4 for k in range(1, 4)]
        self.zs = [self.z] + [(self.z + k) % 8 for k in range(1, 8)]
        self.to_core = (horiz, self.y * 2 + self.other)
        self.to_y = [None] + [(horiz, self.ys[k] * 2 + self.core) for k in range(1, 4)]
        self.to_x = [None] + [(self.xs[k] * 8 + self.z, lev) for k in range(1, 4)]
        self.to_z = [None] + [(self.x * 8 + self.zs[k], lev) for k in range(1, 8)]
        self.peers = [self.to_core] + self.to_y[1:] + self.to_x[1:] + self.to_z[1:]
        self.home = 8 * self.x + self.z
        self.x8 = 8 * self.x
        self.xs8 = [8 * v for v in self.xs]
        self.cell_home = 33 + self.home
        self.cell_x8 = 33 + self.x8
        self.zs2 = [2 * v for v in self.zs]


def sum_phases(place, c_ref, o_ref, bufs, send, recv, cells):
    r0, a0, r1, a1, r2, a2, r3 = bufs
    core, other, x, y, z = place.core, place.other, place.x, place.y, place.z
    sem = iter(range(COPIES))

    def copy(src, dst, peer):
        k = next(sem)
        return lambda: pltpu.make_async_remote_copy(
            src_ref=src, dst_ref=dst, send_sem=send.at[k], recv_sem=recv.at[k],
            device_id=peer, device_id_type=MESH,
        )

    order = (1, 2, 3, 0)
    to_core = [
        copy(c_ref.at[other, place.ys[k]], r0.at[place.ys[k]], place.to_core) for k in order
    ]
    to_y = [copy(a0.at[place.ys[k]], r1.at[k - 1], place.to_y[k]) for k in range(1, 4)]
    to_x, to_z, back_z, back_x = [], [], [], []
    for k in range(1, 4):
        to_x.append(copy(a1.at[pl.ds(place.xs8[k], 8)], r2.at[k - 1, pl.ds(0, 8)], place.to_x[k]))
        to_x.append(copy(a1.at[pl.ds(32, 1)], r2.at[k - 1, pl.ds(8, 1)], place.to_x[k]))
    for k in range(1, 8):
        to_z.append(copy(a2.at[pl.ds(place.zs[k], 1)], r3.at[k - 1, pl.ds(0, 1)], place.to_z[k]))
        to_z.append(copy(a2.at[pl.ds(8, 1)], r3.at[k - 1, pl.ds(1, 1)], place.to_z[k]))
    starts = (place.home, place.cell_home) if cells else (place.home,)
    for k in range(1, 8):
        for s in starts:
            spot = o_ref.at[core, y, pl.ds(s, 1)]
            back_z.append(copy(spot, spot, place.to_z[k]))
    starts = (place.x8, place.cell_x8) if cells else (place.x8,)
    for k in range(1, 4):
        for s in starts:
            spot = o_ref.at[core, y, pl.ds(s, 8)]
            back_x.append(copy(spot, spot, place.to_x[k]))
    spot = o_ref.at[core, y]
    back_y = [copy(spot, spot, place.to_y[k]) for k in range(1, 4)]
    back_core = []
    for k in range(4):
        spot = o_ref.at[core, place.ys_back[k]]
        back_core.append(copy(spot, spot, place.to_core))

    def start(copies):
        for c in copies:
            c().start()

    def arrive(copies):
        for c in copies:
            c().wait_recv()

    def begin():
        start(to_core)

    def add_core():
        for k, c in zip(order, to_core):
            c().wait_recv()
            yk = place.ys[k]
            a0[yk] = c_ref[core, yk] + r0[yk]
            if k:
                to_y[k - 1]().start()

    def add_y():
        arrive(to_y)
        a1[...] = (a0[y] + r1[0]) + (r1[1] + r1[2])
        start(to_x)

    def add_x():
        arrive(to_x)
        a2[0:8] = (a1[pl.ds(place.x8, 8)] + r2[0, 0:8]) + (r2[1, 0:8] + r2[2, 0:8])
        a2[8:9] = (a1[32:33] + r2[0, 8:9]) + (r2[1, 8:9] + r2[2, 8:9])
        start(to_z)

    def add_z():
        arrive(to_z)
        mine = a2[z]
        mean = a2[8]
        for k in range(7):
            mine = mine + r3[k, 0]
            mean = mean + r3[k, 1]
        o_ref[core, y, place.home] = mine
        o_ref[core, y, 32] = mean
        start(back_z)

    def return_x():
        arrive(back_z)
        start(back_x)

    def return_y():
        arrive(back_x)
        start(back_y)
        start(back_core[:1])

    def return_core():
        for k in range(3):
            back_y[k]().wait_recv()
            back_core[k + 1]().start()

    def end():
        arrive(back_core)
        for group in (to_core, to_y, to_x, to_z, back_z, back_x, back_y, back_core):
            for c in group:
                c().wait_send()

    return [begin, add_core, add_y, add_x, add_z, return_x, return_y, return_core, end]


def half_sum_phases(place, c_ref, o_ref, bufs, send, recv):
    r0, a0, r1, a1, r2, a2, r3 = bufs
    core, other, y = place.core, place.other, place.y
    sem = iter(range(COPIES))

    def copy(src, dst, peer):
        k = next(sem)
        return lambda: pltpu.make_async_remote_copy(
            src_ref=src, dst_ref=dst, send_sem=send.at[k], recv_sem=recv.at[k],
            device_id=peer, device_id_type=MESH,
        )

    order = (1, 2, 3, 0)
    to_core = [
        copy(c_ref.at[other, place.ys[k]], r0.at[place.ys[k]], place.to_core) for k in order
    ]
    to_y = [copy(a0.at[place.ys[k]], r1.at[k - 1], place.to_y[k]) for k in range(1, 4)]
    to_z, back_z = [], []
    for k in range(1, 8):
        to_z.append(copy(a1.at[pl.ds(place.zs2[k], 2)], r2.at[k - 1, pl.ds(0, 2)], place.to_z[k]))
        to_z.append(copy(a1.at[pl.ds(16, 1)], r2.at[k - 1, pl.ds(2, 1)], place.to_z[k]))
    to_x = [copy(a2, r3.at[k - 1], place.to_x[k]) for k in range(1, 4)]
    for k in range(1, 8):
        spot = o_ref.at[core, y, pl.ds(place.zs2[0], 2)]
        back_z.append(copy(spot, spot, place.to_z[k]))
    spot = o_ref.at[core, y]
    back_y = [copy(spot, spot, place.to_y[k]) for k in range(1, 4)]
    back_core = []
    for k in range(4):
        spot = o_ref.at[core, place.ys_back[k]]
        back_core.append(copy(spot, spot, place.to_core))

    def start(copies):
        for c in copies:
            c().start()

    def arrive(copies):
        for c in copies:
            c().wait_recv()

    def begin():
        start(to_core)

    def add_core():
        for k, c in zip(order, to_core):
            c().wait_recv()
            yk = place.ys[k]
            a0[yk] = c_ref[core, yk] + r0[yk]
            if k:
                to_y[k - 1]().start()

    def add_y():
        arrive(to_y)
        a1[...] = (a0[y] + r1[0]) + (r1[1] + r1[2])
        start(to_z)

    def add_z():
        arrive(to_z)
        mine = a1[pl.ds(place.zs2[0], 2)]
        mean = a1[16:17]
        for k in range(7):
            mine = mine + r2[k, 0:2]
            mean = mean + r2[k, 2:3]
        a2[0:2] = mine
        a2[2:3] = mean
        start(to_x)

    def add_x():
        arrive(to_x)
        total = (a2[...] + r3[0]) + (r3[1] + r3[2])
        o_ref[core, y, pl.ds(place.zs2[0], 2)] = total[0:2]
        o_ref[core, y, 16] = total[2]
        start(back_z)

    def return_y():
        arrive(back_z)
        start(back_y)
        start(back_core[:1])

    def return_core():
        for k in range(3):
            back_y[k]().wait_recv()
            back_core[k + 1]().start()

    def end():
        arrive(back_core)
        for group in (to_core, to_y, to_z, to_x, back_z, back_y, back_core):
            for c in group:
                c().wait_send()

    return [begin, add_core, add_y, add_z, add_x, return_y, return_core, end]


COPIES = 4 + 3 + 6 + 14 + 14 + 6 + 3 + 4


def sum_buffers():
    def buf(*shape):
        return pltpu.VMEM(shape + (8, B), F32)

    return [buf(4, 33), buf(4, 33), buf(3, 33), buf(33), buf(3, 9), buf(9), buf(7, 2)]


def half_sum_buffers():
    def buf(*shape):
        return pltpu.VMEM(shape + (8, B), F32)

    return [buf(4, 17), buf(4, 17), buf(3, 17), buf(17), buf(7, 3), buf(3), buf(3, 3)]


def factor_block(s, dcol):
    nt = Q // 8
    row = lax.broadcasted_iota(jnp.int32, (8, B), 0)
    lane = lax.broadcasted_iota(jnp.int32, (8, B), 1)
    eye = jnp.where(
        lax.broadcasted_iota(jnp.int32, (B, B), 0) == lax.broadcasted_iota(jnp.int32, (B, B), 1),
        1.0,
        0.0,
    )
    both, shifted = s, eye
    out_a, out_z = [], []
    for o in range(0, B, Q):
        w_t = [both[8 * t : 8 * t + 8] for t in range(nt)]
        z_t = [shifted[8 * t : 8 * t + 8] for t in range(nt)]
        for sub in range(0, Q, SUB):
            begin, end = o + sub, o + sub + SUB
            own = (lane >= begin) & (lane < end)
            cols = {}
            for c in range(sub, sub + SUB):
                cols[c] = [
                    None if t < c // 8 else jnp.broadcast_to(w_t[t][:, o + c : o + c + 1], (8, B))
                    for t in range(nt)
                ]
            for t in range(sub // 8, nt):
                unit = lane == row + (o + 8 * t)
                if t < (sub + SUB) // 8:
                    w_t[t] = jnp.where(own, jnp.where(unit, 1.0, 0.0), w_t[t])
                else:
                    w_t[t] = jnp.where(own, 0.0, w_t[t])
            for r in range(sub, sub + SUB):
                tr, rr = r // 8, r % 8
                p = cols[r][tr][rr : rr + 1]
                rs = lax.rsqrt(p)
                l = [None if t < tr else cols[r][t] * rs for t in range(nt)]
                for c in range(r + 1, sub + SUB):
                    f = l[c // 8][c % 8 : c % 8 + 1]
                    for t in range(c // 8, nt):
                        cols[c][t] = cols[c][t] - l[t] * f
                scale = 1.0 / (p * rs + dcol[o + r : o + r + 1])
                for rows, v in ((w_t, w_t[tr][rr : rr + 1] * rs), (z_t, z_t[tr][rr : rr + 1] * scale)):
                    for t in range(tr, nt):
                        lt = l[t] if t > tr else jnp.where(row > rr, l[t], 0.0)
                        new = rows[t] - lt * v
                        if t == tr:
                            new = jnp.where(row == rr, jnp.broadcast_to(v, (8, B)), new)
                        rows[t] = new
            if sub + SUB < Q:
                ahead = (lane >= end) & (lane < o + Q)
                for t in range(sub // 8, (sub + SUB) // 8):
                    w_t[t] = jnp.where(ahead, 0.0, w_t[t])
        u_b, z_b = jnp.concatenate(w_t, 0), jnp.concatenate(z_t, 0)
        out_a.append(jnp.where(lax.broadcasted_iota(jnp.int32, (Q, B), 1) < o + Q, u_b, 0.0))
        out_z.append(z_b)
        if o + Q < B:
            step = mm(u_b, jnp.concatenate([u_b, z_b], 1), TN)[o + Q :]
            at = lax.broadcasted_iota(jnp.int32, (B - o - Q, B), 1)
            both = jnp.where((at >= o) & (at < o + Q), 0.0, both[Q:]) - step[:, :B]
            shifted = shifted[Q:] - step[:, B:]
    return jnp.concatenate(out_a, 0), jnp.concatenate(out_z, 0)


def rows8(ref, row):
    line = ref[row, :]
    return jnp.concatenate([line[:, k : k + B] for k in range(0, line.shape[1], B)], axis=0)


def analyse(site_of, mean_of, values, variances, damping, x_ref, xm_ref, hooks, between, scratch,
            late):
    (a_ref, yb_ref, p_ref, qs_ref, s_ref, linv_ref, minv_ref, t1_ref, aq_ref, lz_ref,
     d_ref, var_ref, vcol_ref, gt_ref, k_ref) = scratch
    levels, members, cols = x_ref.shape
    n = a_ref.shape[0]
    nb = n // B
    c = 1.0 / (members - 1.0) ** 0.5

    def square(k):
        return lax.broadcasted_iota(jnp.int32, (k, k), 0) == lax.broadcasted_iota(
            jnp.int32, (k, k), 1
        )

    eye_m = jnp.where(square(members), 1.0, 0.0)
    diag = square(B)
    def fill(blocks):
        for i in blocks:
            y_i = site_of(i).T
            a_ref[i * B : (i + 1) * B] = y_i * c
            yb_ref[i * B : (i + 1) * B] = y_i.astype(BF16)
            d_ref[i : i + 1] = values[i : i + 1] - mean_of(i)

    fill(range(nb - late))
    var_ref[...] = variances
    var_cols = columns_of(variances)
    for i in range(nb):
        vcol_ref[i] = jnp.broadcast_to(var_cols[:, i : i + 1], (B, B))
    p_ref[...] = eye_m
    qs_ref[0] = eye_m * (1.0 / c)
    a_0 = a_ref[0:B]
    s_ref[...] = mm(a_0, a_0, NT) + jnp.where(diag, var_ref[0:1], 0.0)
    for ref in (linv_ref, minv_ref, t1_ref, aq_ref):
        ref[...] = jnp.zeros_like(ref)

    def finish_previous(i):
        linv, minv, t1 = linv_ref[...], minv_ref[...], t1_ref[...]
        ip = jnp.maximum(i - 1, 0)
        v = mm(linv, t1)
        z = mm(minv, aq_ref[...])
        lz_ref[rows_at(i)] = mm(linv, z, TN)
        p = p_ref[...] - mm(v, v, TN)
        q = qs_ref[ip] - mm(v, z, TN)
        return p, q

    def step(i, carry):
        p, q = finish_previous(i)
        i_next = jnp.minimum(i + 1, nb - 1)
        a_i = a_ref[rows_at(i)]
        a_n = a_ref[rows_at(i_next)]
        t1 = mm(a_i, p)
        t1_n = mm(a_n, p)
        s_nn = mm(t1_n, a_n, NT) + jnp.where(diag, var_ref[pl.ds(i_next, 1)], 0.0)
        s_in = mm(a_i, t1_n, NT)
        aq = mm(a_i, q)
        linv, minv = factor_block(s_ref[...], jnp.sqrt(vcol_ref[i]))
        l_in = mm(linv, s_in)
        s_ref[...] = s_nn - mm(l_in, l_in, TN)
        linv_ref[...] = linv
        minv_ref[...] = minv
        t1_ref[...] = t1
        aq_ref[...] = aq
        p_ref[...] = p
        qs_ref[i] = q
        for k, hook in enumerate(hooks):
            pl.when(i == k)(hook)
        if late:
            pl.when(i == nb - late - 2)(lambda: fill(range(nb - late, nb)))
        return carry

    lax.fori_loop(0, nb, step, 0)
    p, q = finish_previous(nb)

    d_cols = columns_of(d_ref[...])
    inv_var = [1.0 / vcol_ref[i] for i in range(nb)]

    def over_obs(lines):
        total = 0.0
        for i in range(nb):
            part = a_ref[i * B : (i + 1) * B] * lines[i]
            total = total + jnp.sum(part.reshape(B // 8, 8, members), axis=0)
        return jnp.sum(total, axis=0, keepdims=True)

    def times_a(v):
        return [
            jnp.sum(a_ref[i * B : (i + 1) * B] * v, axis=1, keepdims=True) for i in range(nb)
        ]

    def solve_for(rest):
        v = over_obs([r * inv[:, 0:1] for r, inv in zip(rest, inv_var)])
        back = times_a(mm(jnp.broadcast_to(v, (8, members)), p)[0:1])
        return [(r - t) * inv[:, 0:1] for r, t, inv in zip(rest, back, inv_var)]

    d_lines = [d_cols[:, i : i + 1] for i in range(nb)]
    w_lines = solve_for(d_lines)
    for _ in range(1):
        back = times_a(over_obs(w_lines))
        rest = [
            d - vcol_ref[i][:, 0:1] * w - t
            for i, (d, w, t) in enumerate(zip(d_lines, w_lines, back))
        ]
        w_lines = [w + more for w, more in zip(w_lines, solve_for(rest))]

    for i in range(nb):
        g = lz_ref[(i + 1) * B : (i + 2) * B]
        if i < nb - 1:
            inv = 1.0 / vcol_ref[i]
            g = g - mm(a_ref[i * B : (i + 1) * B], qs_ref[i + 1] - q) * jnp.concatenate([inv, inv], 1)
        gt_ref[:, i * B : (i + 1) * B] = g.T.astype(BF16)

    between(w_lines)
    for lev in range(levels):
        damp_cols = columns_of(damping[lev] * (1.0 / (members - 1.0)))
        slab = x_ref[lev]
        inc, mean = increments(
            lambda i: mm16(yb_ref[i * B : (i + 1) * B], slab) * damp_cols[:, i : i + 1],
            w_lines, gt_ref, k_ref,
        )
        xm_ref[lev : lev + 1] = xm_ref[lev : lev + 1] + mean
        x_ref[lev] = (slab.astype(F32) - inc).astype(BF16)


def increments(gain_of, w_lines, gt_ref, k_ref):
    mean = 0.0
    for i, w in enumerate(w_lines):
        f = gain_of(i)
        k_ref[i * B : (i + 1) * B] = f.astype(BF16)
        mean = mean + jnp.sum((f * w).reshape(B // 8, 8, f.shape[1]), axis=0)
    inc = [mm16(gt_ref[...], k_ref[:, c : c + 256]) for c in range(0, k_ref.shape[1], 256)]
    return jnp.concatenate(inc, axis=1), jnp.sum(mean, axis=0, keepdims=True)


def stack_three(rows):
    hi = rows.astype(BF16)
    mid = (rows - hi.astype(F32)).astype(BF16)
    low = (rows - hi.astype(F32) - mid.astype(F32)).astype(BF16)
    return jnp.concatenate([hi, mid, low], axis=0)


def pick_t(table, hot):
    return lax.dot_general(table, hot, (TN, ((), ())), preferred_element_type=F32)


def update_sites(share_ref, lh_ref, lv_ref, sites, scratch, w_lines, yt_ref, ym_ref, cells_ref):
    tile_ref, col_ref, level_ref, frac_ref = sites
    yb_ref, gt_ref, k_ref = scratch[1], scratch[13], scratch[14]
    n, members = yb_ref.shape
    cols = k_ref.shape[1]
    tiles, levels = lh_ref.shape[1], lv_ref.shape[1]
    lh = stack_three(lh_ref[0] * (1.0 / (members - 1.0)))
    lv = stack_three(lv_ref[0])

    def updated(slab, mean, tile, level):
        hi = slab.astype(BF16)
        low = (slab - hi.astype(F32)).astype(BF16)
        hot_t = one_hot(tiles, tile).astype(BF16)
        hot_l = one_hot(levels, level).astype(BF16)
        hot_t = jnp.concatenate([hot_t] * 3, axis=0)
        hot_l = jnp.concatenate([hot_l] * 3, axis=0)

        def gain_of(i):
            y_i = yb_ref[i * B : (i + 1) * B]
            damp = pick_t(lh[:, i * B : (i + 1) * B], hot_t) * pick_t(lv[:, i * B : (i + 1) * B], hot_l)
            return (mm16(y_i, hi) + mm16(y_i, low)) * damp

        inc, gained = increments(gain_of, w_lines, gt_ref, k_ref)
        return slab - inc, mean + gained

    at = lax.broadcasted_iota(jnp.int32, (8 * tiles, B), 0)
    cell = lax.broadcasted_iota(jnp.int32, (8 * tiles, B), 1)
    t_at, r_at = at // 8, at % 8
    top, bottom, middle = [], [], []
    for pair in range(4):
        parts = [0.0, 0.0, 0.0]
        for core in range(2):
            group = share_ref[core, pair, 33 : 33 + tiles].reshape(8 * tiles, B)
            c = cell - core * 2 * tiles
            lev_at = c // tiles
            hit = (c >= 0) & (c < 2 * tiles) & (c % tiles == t_at)
            for half in range(2):
                sel = jnp.where(hit & (r_at == 2 * lev_at + half), 1.0, 0.0).astype(BF16)
                parts[half] = parts[half] + pick_t(group.astype(BF16), sel)
            sel = jnp.where(hit & (r_at == 4 + lev_at), 1.0, 0.0)
            parts[2] = parts[2] + mm(group, sel, TN)[0:1]
        top.append(parts[0])
        bottom.append(parts[1])
        middle.append(parts[2])
    cells = jnp.concatenate([jnp.concatenate(top, 1), jnp.concatenate(bottom, 1)], 0)
    cell_mean = jnp.concatenate(middle, 1)
    index = lax.broadcasted_iota(jnp.int32, (1, cols), 1)
    cells, cell_mean = updated(cells, cell_mean, index % tiles, index // tiles)
    cells_ref[...] = cells.astype(BF16)
    cell_mean = in_three(cell_mean)
    for half in range(n // cols):
        lanes = slice(half * cols, (half + 1) * cols)
        tile, col, level, frac = (
            ref[1:2, lanes] for ref in (tile_ref, col_ref, level_ref, frac_ref)
        )
        spots = [(p % 2, p // 2) for p in range(4 * half, 4 * half + 4)]
        slab = jnp.concatenate([share_ref[c, y, 0:32].reshape(members, B) for c, y in spots], 1)
        mean = jnp.concatenate([share_ref[c, y, 32][0:1] for c, y in spots], 1)
        slab, mean = updated(slab, mean, tile, level)
        wraps, next_tile, _ = after(tile, col, cols, tiles)
        hot = one_hot(cols, jnp.where(wraps, level * tiles + next_tile, -1)).astype(BF16)
        yt_ref[:, lanes] = slab + frac * mm16(cells_ref[...], hot)
        ym_ref[0:1, lanes] = mean + frac * jnp.sum(mm16(cell_mean, hot)[0:8], axis=0, keepdims=True)


def whole_kernel(*refs):
    args, (x_ref, xm_ref), refs = refs[:10], refs[10:12], refs[12:]
    held, refs = refs[:8], refs[8:]
    share0, panel0, share1, panel1, refs = refs[0], refs[1], refs[2], refs[3], refs[4:]
    bufs0, bufs2, bufs1, refs = refs[:7], refs[7:14], refs[14:21], refs[21:]
    (load, send0, recv0, send2, recv2, send1, recv1), refs = refs[:7], refs[7:]
    (yt_ref, ym_ref, cells_ref), scratch = refs[:3], refs[3:]

    barrier = pltpu.get_barrier_semaphore()
    place = Place()
    for peer in place.peers:
        pl.semaphore_signal(barrier, inc=1, device_id=peer, device_id_type=MESH)
    copies = [
        pltpu.make_async_copy(src, dst, load.at[k])
        for k, (src, dst) in enumerate(zip(args, (x_ref, xm_ref) + tuple(held)))
    ]
    for copy in copies:
        copy.start()
    for copy in copies:
        copy.wait()
    val_ref, var_ref, frac_ref, tile_ref, col_ref, level_ref, lh_ref, lv_ref = held
    sites = (tile_ref, col_ref, level_ref, frac_ref)
    levels, members, cols = x_ref.shape

    def put_first(i, values, mean):
        for half in range(2):
            rows = values[half * B : (half + 1) * B]
            share0[i // 4, half, i % 4, 0:16] = rows.reshape(16, 8, B)
            share0[i // 4, half, i % 4, 16] = mean

    def put_second(i, values, mean):
        share1[i % 2, i // 2, 0:32] = values.reshape(32, 8, B)
        share1[i % 2, i // 2, 32] = mean

    gather_sites(0, True, (0, 1), x_ref, xm_ref, sites, put_first)
    pl.semaphore_wait(barrier, len(place.peers))
    early = half_sum_phases(place, share0.at[0], panel0.at[0], bufs0, send0, recv0)
    later = half_sum_phases(place, share0.at[1], panel0.at[1], bufs2, send2, recv2)
    second_sum = sum_phases(place, share1, panel1, bufs1, send1, recv1, True)
    early[0]()
    gather_sites(0, True, (2, 3), x_ref, xm_ref, sites, put_first)
    later[0]()
    early[1]()
    gather_sites(1, False, range(4), x_ref, xm_ref, sites, put_second)
    r16 = lax.broadcasted_iota(jnp.int32, (B, B), 0)
    own = jnp.zeros((8, B), F32)
    row = lax.broadcasted_iota(jnp.int32, (8, B), 0)
    for lev in range(levels):
        for half in range(2):
            block = x_ref[lev, half * B : (half + 1) * B, 0:B].astype(F32).T
            own = jnp.where(row == 2 * lev + half, block[0:1], own)
        own = jnp.where(row == 4 + lev, xm_ref[lev : lev + 1, 0:1], own)
    panel1[place.core, place.y, place.cell_home] = own
    for k in range(2, 7):
        early[k]()
        later[k - 1]()
    early[7]()
    second_sum[0]()

    def damping(batch):
        near = rows8(lh_ref.at[batch], pl.ds(place.home, 1))
        first = lax.axis_index("lev") * levels
        return [near * rows8(lv_ref.at[batch], pl.ds(first + lev, 1)) for lev in range(levels)]

    def between(w_lines):
        second_sum[8]()
        update_sites(panel1, lh_ref, lv_ref, sites, scratch, w_lines, yt_ref, ym_ref, cells_ref)

    def both(one, two):
        def run():
            one()
            two()
        return run

    hooks = second_sum[1:7] + [lambda: None, second_sum[7]]
    hooks[0] = both(later[6], hooks[0])
    hooks[1] = both(later[7], hooks[1])
    analyse(
        lambda i: jnp.concatenate(
            [panel0[i // 4, half, i % 4, 0:16].reshape(B, B) for half in range(2)], axis=0
        ),
        lambda i: panel0[i // 4, 0, i % 4, 16][0:1],
        rows8(val_ref, slice(0, 1)), rows8(var_ref, slice(0, 1)), damping(0), x_ref, xm_ref,
        hooks, between, scratch, 4,
    )
    analyse(
        lambda i: yt_ref[:, i * B : (i + 1) * B],
        lambda i: ym_ref[0:1, i * B : (i + 1) * B],
        rows8(val_ref, slice(1, 2)), rows8(var_ref, slice(1, 2)), damping(1), x_ref, xm_ref,
        [], lambda w_lines: None, scratch, 0,
    )


def analysis_scratch(n, e, cols):
    nb = n // B

    def buf(*shape):
        return pltpu.VMEM(shape, F32)

    return [
        buf(n, e), pltpu.VMEM((n, e), BF16), buf(e, e), buf(nb + 1, e, e), buf(B, B), buf(B, B),
        buf(B, B), buf(B, e), buf(B, e), buf(n + B, e), buf(nb, B), buf(nb, B),
        buf(nb, B, B), pltpu.VMEM((e, n), BF16), pltpu.VMEM((n, cols), BF16),
    ]


def shards(*args):
    perturb, mean_state, obs_value = args[:3]
    levels, members, cols = perturb.shape
    n = obs_value.shape[1]
    vm = pl.BlockSpec(memory_space=pltpu.VMEM)
    share = pltpu.VMEM((2, 4, members // 8 + 1, 8, B), F32)
    halves = pltpu.VMEM((2, 2, 4, members // 16 + 1, 8, B), F32)
    dma = pltpu.SemaphoreType.DMA
    return pl.pallas_call(
        whole_kernel,
        out_shape=(
            jax.ShapeDtypeStruct(perturb.shape, BF16),
            jax.ShapeDtypeStruct(mean_state.shape, F32),
        ),
        in_specs=[pl.BlockSpec(memory_space=pltpu.HBM)] * len(args),
        out_specs=(vm, vm),
        scratch_shapes=[pltpu.VMEM(a.shape, a.dtype) for a in args[2:]]
        + [halves, halves, share, pltpu.VMEM((2, 4, members // 8 + 33, 8, B), F32)]
        + half_sum_buffers()
        + half_sum_buffers()
        + sum_buffers()
        + [dma((len(args),))] + [dma((COPIES,))] * 6
        + [pltpu.VMEM((members, n), F32), pltpu.VMEM((8, n), F32), pltpu.VMEM((members, cols), BF16)]
        + analysis_scratch(n, members, cols),
        compiler_params=pltpu.CompilerParams(
            collective_id=0, has_side_effects=True, vmem_limit_bytes=60 * 2**20
        ),
        name="analysis",
    )(*args)


def solution(mesh):
    return jax.shard_map(
        shards,
        mesh=mesh,
        in_specs=(P("lev", None, "horiz"), P("lev", "horiz")) + (P(),) * 8,
        out_specs=(P("lev", None, "horiz"), P("lev", "horiz")),
        check_vma=False,
    )
```
